32 devices in a mesh: seq: 8 (over z, y), rep: 4 (over x, core).
Axes of the slice: x: 2, y: 2, z: 4, core: 2. Of those that a mesh axis runs over, the one named last changes fastest.
Arguments:
- hidden_in: bfloat16 [4, 2048, 2048], P('rep', 'seq'), may hold values from -6 to 6
- out_grad: bfloat16 [4, 2048, 2048], P('rep', 'seq'), may hold values from -6 to 6
- segment_ids: int32 [4, 2048], P('rep'), may hold values from 0 to 7, never falling along the last dimension, each value on 1 to 512 neighbouring positions
- row_position: int32 [4, 2048], P('rep'), may hold values from 0 to 2047, as said below
- gain_first: bfloat16 [2048], P('seq'), may hold values from 0.5 to 1.5
- shift_first: bfloat16 [2048], P('seq'), may hold values from -1.5 to 1.5
- qkv_weight: bfloat16 [2048, 2304], P('seq'), may hold values from -0.1875 to 0.1875
- qv_bias: bfloat16 [2176], P('seq'), may hold values from -2.5 to 2.5
- out_weight: bfloat16 [2048, 2048], P('seq'), may hold values from -0.375 to 0.375
- out_bias: bfloat16 [2048], P('seq'), may hold values from -2.5 to 2.5
- gain_second: bfloat16 [2048], P('seq'), may hold values from 0.5 to 1.5
- shift_second: bfloat16 [2048], P('seq'), may hold values from -1.5 to 1.5
- fc_weight: bfloat16 [2048, 8192], P('seq'), may hold values from -0.125 to 0.125
- fc_bias: bfloat16 [8192], P('seq'), may hold values from -2.5 to 2.5
- proj_weight: bfloat16 [8192, 2048], P('seq'), may hold values from -0.0625 to 0.0625
- proj_bias: bfloat16 [2048], P('seq'), may hold values from -2.5 to 2.5
Outputs:
- hidden_out: bfloat16 [4, 2048, 2048], P('rep', 'seq')
- input_grad: float32 [4, 2048, 2048], P('rep', 'seq')
- dgain_first: float32 [2048], P('seq')
- dshift_first: float32 [2048], P('seq')
- dqkv_weight: float32 [2048, 2304], P('seq')
- dqv_bias: float32 [2176], P('seq')
- dout_weight: float32 [2048, 2048], P('seq')
- dout_bias: float32 [2048], P('seq')
- dgain_second: float32 [2048], P('seq')
- dshift_second: float32 [2048], P('seq')
- dfc_weight: float32 [2048, 8192], P('seq')
- dfc_bias: float32 [8192], P('seq')
- dproj_weight: float32 [8192, 2048], P('seq')
- dproj_bias: float32 [2048], P('seq')
The draws below stay inside these ranges and needn't reach their ends.
Inputs may be any that keep to these rules, and one draw needn't show every extreme that they name: `row_position`: in each window the values form a permutation of 0 to 2047. Of the 256 stored rows with indices in [j * 256, (j + 1) * 256), at most 64 have places in [k * 256, (k + 1) * 256) for any k, and for every j exactly 64 do for one k. `segment_ids`: segment numbers never fall along a window's sequence order; each segment has at most 512 places.
All inputs are finite; a program needn't handle non-finite values.
Results may differ from the reference program's by a relative error of at most 0.02.
Values may be sent and summed in bfloat16 or wider, within the bound.
No kernel may reach another device: no remote copies, remote signals or barrier semaphores. Data moves between devices by JAX's collectives and lax.ppermute only.
A program may use at most 384 MiB of HBM per device.

```python
import math
import jax
import jax.numpy as jnp
import numpy as np
from jax import lax

D = 2048
HEADS = 16
HD = 128
FF = 8192
TOK_DEV = 256
KBLK = 512
WINDOWS = 4
W = 2048
SEGS = 8
DOC_MAX = 512


def draw_row_position(key, part):
    blocks = W // TOK_DEV
    per_pair = TOK_DEV // blocks

    def one_window(window_key):
        subkeys = jax.random.split(window_key, 6)
        row_perm = jax.random.permutation(subkeys[0], blocks).astype(jnp.int32)
        col_perm = jax.random.permutation(subkeys[1], blocks).astype(jnp.int32)
        swings = jax.random.randint(subkeys[2], (blocks // 2,), 0, per_pair + 1, dtype=jnp.int32)
        swings = swings.at[0].set(per_pair)
        levels = jnp.concatenate([per_pair + swings, per_pair - swings]).astype(jnp.int32)
        levels = levels[jax.random.permutation(subkeys[3], blocks).astype(jnp.int32)]
        latin_sq = (row_perm[:, None] + col_perm[None, :]) % blocks
        counts = levels[latin_sq]
        upper_cum = jnp.cumsum(counts, axis=1)
        slot_ids = jnp.arange(TOK_DEV, dtype=jnp.int32)
        ordered = jnp.sum((slot_ids[None, :, None] >= upper_cum[:, None, :]).astype(jnp.int32), axis=2)
        mixers = jax.vmap(lambda k: jax.random.permutation(k, TOK_DEV))(jax.random.split(subkeys[4], blocks)).astype(jnp.int32)
        targets = jnp.take_along_axis(ordered, mixers, axis=1)
        lane_ids = jnp.arange(blocks, dtype=jnp.int32)
        onehot = (targets[:, :, None] == lane_ids[None, None, :]).astype(jnp.int32)
        rank_ids = jnp.sum((jnp.cumsum(onehot, axis=1) - onehot) * onehot, axis=2)
        offsets = jnp.cumsum(counts, axis=0) - counts
        within = jnp.take_along_axis(offsets, targets, axis=1) + rank_ids
        inside = jax.vmap(lambda k: jax.random.permutation(k, TOK_DEV))(jax.random.split(subkeys[5], blocks)).astype(jnp.int32)
        placed = targets * TOK_DEV + inside[targets, within]
        return placed.reshape(blocks * TOK_DEV).astype(jnp.int32)
    return jax.vmap(one_window)(jax.random.split(key, WINDOWS))


def level_of(key, shape, cuts, least, top_value):
    gain = 1.0
    for axis_at, shards_of in cuts:
        draws = jax.random.uniform(jax.random.fold_in(jax.random.fold_in(key, 6), axis_at), (shards_of,), jnp.float32, least / len(cuts), top_value / len(cuts))
        gain = gain * jnp.repeat(jnp.exp(draws), shape[axis_at] // shards_of).reshape((-1,) + (1,) * (len(shape) - 1 - axis_at))
    return gain


def length_profile(count, total, most, slope):
    weights = [(1 << 20) // math.isqrt(grade ** slope) + 1 for grade in range(2, count + 1)]
    rest, holding = total - most - (count - 1), [1] * (count - 1)
    while rest > 0:
        movable = [i for i in range(count - 1) if holding[i] < most]
        pool, left = sum([weights[i] for i in movable]), rest
        for i in movable:
            more = min(most - holding[i], max(1, left * weights[i] // pool), rest)
            holding[i] = holding[i] + more
            rest = rest - more
    return np.array([most] + holding)


def ragged_sizes(stream_key, amount, total, bound, slope):
    if amount == 2:
        one = jax.random.randint(stream_key, (), max(1, total - bound), min(bound, total - 1) + 1)
        return jnp.stack([one, total - one])
    tallies = jnp.asarray(length_profile(amount, total, bound, slope), jnp.int32)
    pairs = (amount - 1) // 2
    source_of, sink = tallies[1:1 + 2 * pairs:2], tallies[2:2 + 2 * pairs:2]
    room = jnp.minimum(source_of - 1, bound - sink)
    moved = jax.random.randint(jax.random.fold_in(stream_key, 1), (pairs,), 0, 1 << 20) % (room + 1)
    tallies = tallies.at[1:1 + 2 * pairs:2].set(source_of - moved).at[2:2 + 2 * pairs:2].set(sink + moved)
    return tallies[jax.random.permutation(jax.random.fold_in(stream_key, 2), amount)]


def normal_values(key, shape, scale, most, cuts=(), kind=jnp.bfloat16):
    loudness = level_of(key, shape, cuts, -0.22, 0.18) if cuts else 1.0
    drawn = jax.random.normal(key, shape, jnp.float32) * scale * loudness
    return jnp.minimum(jnp.maximum(drawn, -most), most).astype(kind)


def setup_inputs(seed: int = 0) -> dict:
    key_of = jax.random.split(jax.random.key(seed), 17)
    hidden_in = normal_values(key_of[0], (WINDOWS, W, D), 1.0, 6.0, ((0, 4), (1, 8)))
    out_grad = normal_values(key_of[1], (WINDOWS, W, D), 1.0, 6.0, ((0, 4), (1, 8)))
    segment_ids = jax.vmap(lambda own: jnp.searchsorted(jnp.cumsum(ragged_sizes(own, SEGS, W, DOC_MAX, 2)), jnp.arange(W), side="right"))(jax.random.split(key_of[2], WINDOWS)).reshape((WINDOWS, W)).astype(jnp.int32)
    row_position = draw_row_position(jax.random.fold_in(key_of[16], 71), 0)
    gain_first = jnp.clip(1.0 + 0.1 * jax.random.normal(key_of[4], (D,), jnp.float32), 0.5, 1.5).astype(jnp.bfloat16)
    shift_first = normal_values(key_of[5], (D,), 0.3, 1.5, ((0, 8),))
    qkv_weight = normal_values(key_of[6], (D, D + 2 * HD), (D // 2) ** -0.5, 0.1875, ((0, 8),))
    qv_bias = normal_values(key_of[7], (D + HD,), 0.5, 2.5, ((0, 8),))
    out_weight = normal_values(key_of[8], (D, D), (D // 8) ** -0.5, 0.375, ((0, 8),))
    out_bias = normal_values(key_of[9], (D,), 0.5, 2.5, ((0, 8),))
    gain_second = jnp.clip(1.0 + 0.1 * jax.random.normal(key_of[10], (D,), jnp.float32), 0.5, 1.5).astype(jnp.bfloat16)
    shift_second = normal_values(key_of[11], (D,), 0.3, 1.5, ((0, 8),))
    fc_weight = normal_values(key_of[12], (D, FF), D ** -0.5, 0.125, ((0, 8),))
    fc_bias = normal_values(key_of[13], (FF,), 0.5, 2.5, ((0, 8),))
    proj_weight = normal_values(key_of[14], (FF, D), FF ** -0.5, 0.0625, ((0, 8),))
    proj_bias = normal_values(key_of[15], (D,), 0.5, 2.5, ((0, 8),))
    return {"hidden_in": hidden_in, "out_grad": out_grad, "segment_ids": segment_ids, "row_position": row_position, "gain_first": gain_first, "shift_first": shift_first, "qkv_weight": qkv_weight, "qv_bias": qv_bias, "out_weight": out_weight, "out_bias": out_bias, "gain_second": gain_second, "shift_second": shift_second, "fc_weight": fc_weight, "fc_bias": fc_bias, "proj_weight": proj_weight, "proj_bias": proj_bias}


EPSILON = 1e-05
NEGATIVE = -1e+30

@jax.custom_vjp
def low(v):
    return lax.optimization_barrier(v.astype(jnp.bfloat16)).astype(jnp.float32)

@jax.custom_vjp
def low_back(v):
    return v

def low_keep(v):
    return (low(v), None)

def low_pass(kept, grad):
    return (grad,)

def back_keep(v):
    return (v, None)

def back_low(kept, grad):
    return (low(grad),)
low.defvjp(low_keep, low_pass)
low_back.defvjp(back_keep, back_low)

def matmul_high(left, right):
    return jnp.dot(left, right, precision=lax.Precision.HIGHEST, preferred_element_type=jnp.float32)

def layer_norm(values, gain_vec, shift_vec):
    center = values - lax.optimization_barrier(jnp.mean(values, axis=-1, keepdims=True))
    spread = lax.optimization_barrier(jnp.mean(center * center, axis=-1, keepdims=True))
    return center * lax.rsqrt(spread + EPSILON) * gain_vec + shift_vec

def gelu_tanh(values):
    tanh_arg = math.sqrt(2.0 / math.pi) * (values + 0.044715 * values * values * values)
    return 0.5 * values * (1.0 + jnp.tanh(tanh_arg))

def window_attention(queries, keys_win, values_win, segments):
    places = jnp.arange(W, dtype=jnp.int32)
    live_mask = segments != SEGS - 1

    def one_block(block_id):
        first_row = block_id * KBLK
        query_rows = lax.dynamic_slice_in_dim(queries, first_row, KBLK)
        query_places = first_row + jnp.arange(KBLK, dtype=jnp.int32)
        query_segments = lax.dynamic_slice_in_dim(segments, first_row, KBLK)
        query_live = lax.dynamic_slice_in_dim(live_mask, first_row, KBLK)
        raw_scores = low_back(jnp.einsum('thd,ud->thu', query_rows, keys_win, precision=lax.Precision.HIGHEST))
        scores = raw_scores * (1.0 / math.sqrt(HD))
        allowed = (query_segments[:, None] == segments[None, :]) & (places[None, :] <= query_places[:, None]) & query_live[:, None]
        allowed = allowed[:, None, :]
        masked = jnp.where(allowed, scores, NEGATIVE)
        row_max = lax.optimization_barrier(jnp.max(masked, axis=-1, keepdims=True))
        exp_weights = jnp.exp(masked - row_max) * allowed.astype(jnp.float32)
        row_sums = lax.optimization_barrier(jnp.sum(exp_weights, axis=-1))
        row_sums = jnp.where(query_live[:, None], row_sums, 1.0)
        mixed = jnp.einsum('thu,ud->thd', low(exp_weights), values_win, precision=lax.Precision.HIGHEST)
        return mixed / row_sums[:, :, None] * query_live[:, None, None].astype(jnp.float32)
    blocks = lax.map(jax.checkpoint(one_block), jnp.arange(W // KBLK, dtype=jnp.int32))
    return blocks.reshape(W, HEADS * HD)

def forward(hidden, gain_first, shift_first, qkv_weight, qv_bias, out_weight, out_bias, gain_second, shift_second, fc_weight, fc_bias, proj_weight, proj_bias, row_position, segment_ids):
    rows_all = hidden.reshape(WINDOWS * W, D)
    normed_one = low(layer_norm(rows_all, gain_first, shift_first))
    projected = matmul_high(normed_one, qkv_weight)
    queries = low(low_back(projected[:, :D] + qv_bias[:D]))
    keys_all = low(low_back(projected[:, D:D + HD]))
    values_all = low(low_back(projected[:, D + HD:] + qv_bias[D:]))
    inverse = jax.vmap(lambda p: jnp.zeros((W,), jnp.int32).at[p].set(jnp.arange(W, dtype=jnp.int32)))(row_position)

    def attend(window_parts):
        query_win, key_win, value_win, inverse_win, segment_win, place_win = window_parts
        in_order = window_attention(query_win[inverse_win].reshape(W, HEADS, HD), key_win[inverse_win], value_win[inverse_win], segment_win)
        return in_order[place_win]
    attended = lax.map(attend, (queries.reshape(WINDOWS, W, D), keys_all.reshape(WINDOWS, W, HD), values_all.reshape(WINDOWS, W, HD), inverse, segment_ids, row_position))
    attended = low(low_back(attended.reshape(WINDOWS * W, D)))
    branch = low_back(matmul_high(attended, out_weight) + out_bias)
    middle = rows_all + branch
    normed_two = low(layer_norm(middle, gain_second, shift_second))
    pre_act = low_back(matmul_high(normed_two, fc_weight) + fc_bias)
    activated = low(gelu_tanh(pre_act))
    result = middle + matmul_high(activated, proj_weight) + proj_bias
    return result.reshape(WINDOWS, W, D)

def reference(hidden_in, out_grad, segment_ids, row_position, gain_first, shift_first, qkv_weight, qv_bias, out_weight, out_bias, gain_second, shift_second, fc_weight, fc_bias, proj_weight, proj_bias):
    params = [gain_first, shift_first, qkv_weight, qv_bias, out_weight, out_bias, gain_second, shift_second, fc_weight, fc_bias, proj_weight, proj_bias]
    params = [item.astype(jnp.float32) for item in params]

    def wrapped(hidden, *weights):
        return forward(hidden, *weights, row_position, segment_ids)
    result, pullback = jax.vjp(wrapped, hidden_in.astype(jnp.float32), *params)
    grads = pullback(out_grad.astype(jnp.float32))
    return (result.astype(jnp.bfloat16), grads[0], grads[1], grads[2], grads[3], grads[4], grads[5], grads[6], grads[7], grads[8], grads[9], grads[10], grads[11], grads[12])
```

```python
import functools
import math

import jax
import jax.numpy as jnp
from jax import lax
from jax.experimental import pallas as pl
from jax.experimental.pallas import tpu as pltpu
from jax.sharding import Mesh
from jax.sharding import PartitionSpec as P

HD = 128
EPSILON = 1e-05
NEGATIVE = -1e30
SCALE = 1.0 / math.sqrt(HD)
LOG2E = math.log2(math.e)
GELU_C = math.sqrt(2.0 / math.pi)
SEQ = ("z", "y")
REP = ("x", "c")
PLANE = ("y", "x", "c")
ALL = ("z", "y", "x", "c")
BF16 = jnp.bfloat16
F32 = jnp.float32
HEADS_STEP = 2


def dot(left, right, dims):
    return lax.dot_general(left, right, (dims, ((), ())), preferred_element_type=F32)


NN = ((1,), (0,))
NT = ((1,), (1,))
TN = ((0,), (0,))


def attention_bias(seg_own, seg_ctx, padding_id, rows, ctx):
    t = lax.broadcasted_iota(jnp.int32, (rows, ctx), 0)
    u = lax.broadcasted_iota(jnp.int32, (rows, ctx), 1)
    allowed = (seg_own == seg_ctx) & (u <= t + (ctx - rows)) & (seg_own != padding_id)
    return jnp.where(allowed, 0.0, NEGATIVE).astype(F32)


def forward_kernel(padding_id, q_ref, kv_ref, own_ref, ctx_ref, low_ref, att_ref, norm_ref, bias):
    rows, ctx = bias.shape

    @pl.when(pl.program_id(0) == 0)
    def _():
        bias[...] = attention_bias(own_ref[...], ctx_ref[...], padding_id, rows, ctx)

    live = own_ref[...] != padding_id
    keys = kv_ref[:, :HD]
    values = kv_ref[:, HD:]
    for head in range(HEADS_STEP):
        lanes = slice(head * HD, (head + 1) * HD)
        scores = dot(q_ref[:, lanes], keys, NT) * (SCALE * LOG2E) + bias[...]
        top = jnp.max(scores, axis=1, keepdims=True)
        weights = jnp.exp2(scores - top)
        sums = jnp.sum(weights, axis=1, keepdims=True)
        mixed = dot(weights.astype(BF16), values, NN)
        attended = jnp.where(live, mixed / sums, 0.0)
        att_ref[:, lanes] = attended
        low_ref[:, lanes] = attended.astype(BF16)
        norm = jnp.where(live, top + jnp.log2(sums), 0.0)
        norm_ref[:, lanes] = jnp.broadcast_to(norm, (rows, HD))


def attention_forward(queries, kv_ctx, seg_own, seg_ctx, padding_id):
    rows, width = queries.shape
    ctx = kv_ctx.shape[0]
    step = HEADS_STEP * HD
    tile = pl.BlockSpec((rows, step), lambda h: (0, h))
    return pl.pallas_call(
        functools.partial(forward_kernel, padding_id),
        grid=(width // step,),
        in_specs=[
            tile,
            pl.BlockSpec((ctx, 2 * HD), lambda h: (0, 0)),
            pl.BlockSpec((rows, 1), lambda h: (0, 0)),
            pl.BlockSpec((1, ctx), lambda h: (0, 0)),
        ],
        out_specs=[tile, tile, tile],
        out_shape=[
            jax.ShapeDtypeStruct((rows, width), BF16),
            jax.ShapeDtypeStruct((rows, width), F32),
            jax.ShapeDtypeStruct((rows, width), F32),
        ],
        scratch_shapes=[pltpu.VMEM((rows, ctx), F32)],
        compiler_params=pltpu.CompilerParams(vmem_limit_bytes=40 * 1024 * 1024),
        cost_estimate=pl.CostEstimate(
            flops=4 * rows * ctx * width,
            bytes_accessed=12 * rows * width,
            transcendentals=rows * ctx * width // HD,
        ),
        name="attention_forward",
    )(queries, kv_ctx, seg_own, seg_ctx)


def backward_kernel(
    padding_id, q_ref, g_ref, att_ref, norm_ref, kv_ref, own_ref, ctx_ref, dq_ref, dkv_ref, bias
):
    rows, ctx = bias.shape

    @pl.when(pl.program_id(0) == 0)
    def _():
        bias[...] = attention_bias(own_ref[...], ctx_ref[...], padding_id, rows, ctx)
        dkv_ref[...] = jnp.zeros_like(dkv_ref)

    keys = kv_ref[:, :HD]
    values = kv_ref[:, HD:]
    for head in range(HEADS_STEP):
        lanes = slice(head * HD, (head + 1) * HD)
        q = q_ref[:, lanes]
        g = g_ref[:, lanes]
        delta = jnp.sum(g.astype(F32) * att_ref[:, lanes], axis=1, keepdims=True)
        norm = norm_ref[:, head * HD : head * HD + 1]
        scores = dot(q, keys, NT) * (SCALE * LOG2E) + bias[...]
        prob = jnp.exp2(scores - norm)
        grad_prob = dot(g, values, NT)
        grad_scores = (prob * (grad_prob - delta) * SCALE).astype(BF16)
        dq_ref[:, lanes] = dot(grad_scores, keys, NN).astype(BF16)
        dkv_ref[:, :HD] += dot(grad_scores, q, TN)
        dkv_ref[:, HD:] += dot(prob.astype(BF16), g, TN)


def attention_backward(queries, grads, attended, norms, kv_ctx, seg_own, seg_ctx, padding_id):
    rows, width = queries.shape
    ctx = kv_ctx.shape[0]
    step = HEADS_STEP * HD
    tile = pl.BlockSpec((rows, step), lambda h: (0, h))
    whole = pl.BlockSpec((ctx, 2 * HD), lambda h: (0, 0))
    return pl.pallas_call(
        functools.partial(backward_kernel, padding_id),
        grid=(width // step,),
        in_specs=[
            tile,
            tile,
            tile,
            tile,
            whole,
            pl.BlockSpec((rows, 1), lambda h: (0, 0)),
            pl.BlockSpec((1, ctx), lambda h: (0, 0)),
        ],
        out_specs=[tile, whole],
        out_shape=[
            jax.ShapeDtypeStruct((rows, width), BF16),
            jax.ShapeDtypeStruct((ctx, 2 * HD), F32),
        ],
        scratch_shapes=[pltpu.VMEM((rows, ctx), F32)],
        compiler_params=pltpu.CompilerParams(vmem_limit_bytes=48 * 1024 * 1024),
        cost_estimate=pl.CostEstimate(
            flops=10 * rows * ctx * width,
            bytes_accessed=14 * rows * width,
            transcendentals=rows * ctx * width // HD,
        ),
        name="attention_backward",
    )(queries, grads, attended, norms, kv_ctx, seg_own, seg_ctx)


def norm_parts(values):
    center = values - jnp.mean(values, axis=-1, keepdims=True)
    spread = jnp.mean(center * center, axis=-1, keepdims=True)
    rstd = lax.rsqrt(spread + EPSILON)
    return center * rstd, rstd


def norm_back(grad, unit, rstd, gain):
    scaled = grad * gain
    mean_g = jnp.mean(scaled, axis=-1, keepdims=True)
    mean_gu = jnp.mean(scaled * unit, axis=-1, keepdims=True)
    return rstd * (scaled - mean_g - unit * mean_gu)


def gelu_pair(v):
    inner = jnp.tanh(GELU_C * (v + 0.044715 * v * v * v))
    value = 0.5 * v * (1.0 + inner)
    slope = 0.5 * (1.0 + inner) + 0.5 * v * (1.0 - inner * inner) * GELU_C * (
        1.0 + 3.0 * 0.044715 * v * v
    )
    return value, slope


def gather_plane(block):
    return lax.all_gather(block, PLANE, axis=0, tiled=True)


def scatter_plane(partial):
    return lax.psum_scatter(partial, PLANE, scatter_dimension=0, tiled=True)


def shards(
    hidden_in,
    out_grad,
    segment_ids,
    row_position,
    gain_first,
    shift_first,
    qkv_weight,
    qv_bias,
    out_weight,
    out_bias,
    gain_second,
    shift_second,
    fc_weight,
    fc_bias,
    proj_weight,
    proj_bias,
):
    zs, ys, xs, cs = (lax.axis_size(a) for a in ALL)
    reps = xs * cs
    plane = ys * reps
    seqs = zs * ys
    z_at = lax.axis_index("z")
    y_at = lax.axis_index("y")
    q_at = lax.axis_index("x") * cs + lax.axis_index("c")
    f_at = y_at * reps + q_at
    seq_at = z_at * ys + y_at
    rows = hidden_in.shape[1]
    width = hidden_in.shape[2]
    window = rows * seqs
    capacity = 2 * rows // seqs
    slots = seqs * capacity
    halo = max(1, seqs // 4)
    ctx = (halo + 1) * rows
    padding_id = max(8, window // 256) - 1
    qkv_cols = qkv_weight.shape[1]
    ff = fc_weight.shape[1]
    ff_block = ff // seqs
    ff_unit = ff_block // reps
    ff_own = zs * ff_unit

    places = row_position[0]
    segments = segment_ids[0]
    targets = (places // rows).reshape(seqs, rows)
    earlier = (
        lax.broadcasted_iota(jnp.int32, (rows, rows), 1)
        < lax.broadcasted_iota(jnp.int32, (rows, rows), 0)
    )
    same = (targets[:, :, None] == targets[:, None, :]) & earlier[None]
    ranks = jnp.sum(same.astype(jnp.int32), axis=2).reshape(window)
    first_row = seq_at * rows
    own_places_stored = lax.dynamic_slice_in_dim(places, first_row, rows)
    own_ranks = lax.dynamic_slice_in_dim(ranks, first_row, rows)
    send_slots = own_places_stored // rows * capacity + own_ranks
    arrive_slots = jnp.arange(window, dtype=jnp.int32) // rows * capacity + ranks
    own_places = first_row + jnp.arange(rows, dtype=jnp.int32)
    recv_slots = jnp.sum(
        jnp.where(places[None, :] == own_places[:, None], arrive_slots[None, :], 0), axis=1
    )
    slot_ids = jnp.arange(slots, dtype=jnp.int32)
    pick_send = (send_slots[:, None] == slot_ids[None, :]).astype(BF16)
    pick_recv = (recv_slots[:, None] == slot_ids[None, :]).astype(BF16)

    def exchange(values, pick_out, pick_in):
        packed = dot(pick_out, values, TN).astype(BF16).reshape(seqs, capacity, values.shape[1])
        moved = lax.all_to_all(packed, SEQ, split_axis=0, concat_axis=0, tiled=True)
        return dot(pick_in, moved.reshape(slots, values.shape[1]), NN)

    def to_places(values):
        return exchange(values, pick_send, pick_recv)

    def to_stored(values):
        return exchange(values, pick_recv, pick_send)

    small = jnp.concatenate(
        [gain_first, shift_first, qv_bias, out_bias, gain_second, shift_second, fc_bias, proj_bias]
    )
    small_all = lax.all_gather(small, SEQ, axis=0, tiled=True).reshape(seqs, -1).astype(F32)
    parts = []
    at = 0
    for item in (
        gain_first,
        shift_first,
        qv_bias,
        out_bias,
        gain_second,
        shift_second,
        fc_bias,
        proj_bias,
    ):
        parts.append(small_all[:, at : at + item.shape[0]].reshape(-1))
        at += item.shape[0]
    gain1, shift1, qv_full, out_shift, gain2, shift2, fc_shift, proj_shift = parts
    fc_shift_own = lax.dynamic_slice(
        fc_shift.reshape(zs, ys, reps, ff_unit), (0, y_at, q_at, 0), (zs, 1, 1, ff_unit)
    ).reshape(ff_own)

    def quarter(weight, axis):
        size = weight.shape[axis] // reps
        return lax.dynamic_slice_in_dim(weight, q_at * size, size, axis)

    full_qkv = lax.all_gather(quarter(qkv_weight, 0), ALL, axis=0, tiled=True)
    full_out = lax.all_gather(quarter(out_weight, 0), ALL, axis=0, tiled=True)
    proj_own = lax.all_gather(quarter(proj_weight, 0), "z", axis=0, tiled=True)
    fc_view = fc_weight.reshape(width // seqs, zs, ys, reps, ff_unit)
    fc_quarter = lax.dynamic_slice_in_dim(fc_view, q_at, 1, 3)[:, :, :, 0]
    fc_send = fc_quarter.transpose(2, 0, 1, 3).reshape(ys, width // seqs, ff_own)
    fc_pair = lax.all_to_all(fc_send, "y", split_axis=0, concat_axis=0, tiled=True)
    fc_own = lax.all_gather(
        fc_pair.reshape(ys * (width // seqs), ff_own), "z", axis=0, tiled=True
    )

    inputs = to_places(hidden_in[0])
    unit1, rstd1 = norm_parts(inputs)
    normed1 = (unit1 * gain1 + shift1).astype(BF16)
    projected = dot(normed1, full_qkv, NN)
    queries = (projected[:, :width] + qv_full[:width]).astype(BF16)
    kv_shift = jnp.concatenate([jnp.zeros((HD,), F32), qv_full[width:]])
    kv_own = (projected[:, width:] + kv_shift).astype(BF16)
    blocks = []
    for back in range(halo, 0, -1):
        pairs = [(i, i + back) for i in range(seqs - back)]
        blocks.append(lax.ppermute(kv_own, SEQ, pairs))
    kv_ctx = jnp.concatenate(blocks + [kv_own], axis=0)
    seg_own = lax.dynamic_slice_in_dim(segments, first_row, rows)[:, None]
    seg_padded = jnp.concatenate([jnp.full((halo * rows,), -1, jnp.int32), segments])
    seg_ctx = lax.dynamic_slice_in_dim(seg_padded, first_row, ctx)[None, :]
    attended_low, attended, norms = attention_forward(
        queries, kv_ctx, seg_own, seg_ctx, padding_id
    )
    middle = inputs + (dot(attended_low, full_out, NN) + out_shift)

    unit2, rstd2 = norm_parts(middle)
    normed2 = (unit2 * gain2 + shift2).astype(BF16)
    grad_f32 = to_places(out_grad[0])
    grad_low = grad_f32.astype(BF16)
    grad_all = gather_plane(grad_low)
    normed2_all = gather_plane(normed2)
    pre_act = dot(normed2_all, fc_own, NN) + fc_shift_own
    act, slope = gelu_pair(pre_act)
    act_low = act.astype(BF16)
    mlp_out = scatter_plane(dot(act_low, proj_own, NN).astype(BF16))
    result = (middle + mlp_out.astype(F32) + proj_shift).astype(BF16)
    hidden_out = to_stored(result).astype(BF16)
    grad_pre = (dot(grad_all, proj_own, NT) * slope).astype(BF16)
    grad_normed2 = scatter_plane(dot(grad_pre, fc_own, NT).astype(BF16)).astype(F32)
    dfc_bias_own = jnp.sum(grad_pre.astype(F32), axis=0)
    dproj_own = dot(act_low, grad_all, TN).astype(BF16)
    dfc_own = dot(normed2_all, grad_pre, TN).astype(BF16)
    dgain2 = jnp.sum(grad_normed2 * unit2, axis=0)
    dshift2 = jnp.sum(grad_normed2, axis=0)
    dproj_bias = jnp.sum(grad_f32, axis=0)
    grad_middle = grad_f32 + norm_back(grad_normed2, unit2, rstd2, gain2)

    grad_branch = grad_middle.astype(BF16)
    dout_bias = jnp.sum(grad_branch.astype(F32), axis=0)
    grad_attended = dot(grad_branch, full_out, NT).astype(BF16)
    dq, dkv_ctx = attention_backward(
        queries, grad_attended, attended, norms, kv_ctx, seg_own, seg_ctx, padding_id
    )
    dkv = dkv_ctx[halo * rows :]
    for back in range(1, halo + 1):
        pairs = [(i + back, i) for i in range(seqs - back)]
        term = dkv_ctx[(halo - back) * rows : (halo - back + 1) * rows].astype(BF16)
        dkv = dkv + lax.ppermute(term, SEQ, pairs).astype(F32)
    grad_qkv = jnp.concatenate([dq, dkv.astype(BF16)], axis=1)
    grad_normed1 = dot(grad_qkv, full_qkv, NT)
    dgain1 = jnp.sum(grad_normed1 * unit1, axis=0)
    dshift1 = jnp.sum(grad_normed1, axis=0)
    grad_in = grad_middle + norm_back(grad_normed1, unit1, rstd1, gain1)
    input_grad = to_stored(grad_in.astype(BF16))
    grad_qkv_f32 = grad_qkv.astype(F32)
    dqv_bias = jnp.concatenate(
        [jnp.sum(grad_qkv_f32[:, :width], axis=0), jnp.sum(grad_qkv_f32[:, width + HD :], axis=0)]
    )

    def columns_of_plane(values):
        cols = values.shape[1] // plane
        sent = values.reshape(rows, plane, cols).transpose(1, 0, 2)
        return lax.all_to_all(sent, PLANE, split_axis=0, concat_axis=0, tiled=True).reshape(
            plane * rows, cols
        )

    normed1_all = gather_plane(normed1)
    attended_all = gather_plane(attended_low)
    dout_own = dot(attended_all, columns_of_plane(grad_branch), TN).astype(BF16)
    dqkv_own = dot(normed1_all, columns_of_plane(grad_qkv), TN).astype(BF16)

    def over_z(partial):
        return lax.psum_scatter(partial, "z", scatter_dimension=0, tiled=True)

    def by_rows(partial):
        cols = partial.shape[1]
        mine = lax.all_to_all(
            partial.reshape(ys, -1, cols), "y", split_axis=0, concat_axis=0, tiled=True
        )
        return lax.all_gather(mine, REP, axis=0, tiled=False).reshape(reps, ys, -1, cols)

    dproj_weight = lax.all_gather(over_z(dproj_own), REP, axis=0, tiled=True).astype(F32)
    dfc_rows = by_rows(over_z(dfc_own)).reshape(reps, ys, width // seqs, zs, ff_unit)
    dfc_weight = dfc_rows.transpose(2, 3, 1, 0, 4).reshape(width // seqs, ff).astype(F32)
    dout_rows = by_rows(over_z(dout_own))
    dout_weight = dout_rows.transpose(2, 1, 0, 3).reshape(width // seqs, width).astype(F32)
    dqkv_rows = by_rows(over_z(dqkv_own))
    dqkv_weight = dqkv_rows.transpose(2, 1, 0, 3).reshape(width // seqs, qkv_cols).astype(F32)

    dfc_bias = lax.dynamic_update_slice(
        jnp.zeros((zs, ys, reps, ff_unit), F32),
        dfc_bias_own.reshape(zs, 1, 1, ff_unit),
        (0, y_at, q_at, 0),
    ).reshape(ff)
    mids = (dout_bias, dgain2, dshift2, dfc_bias, dproj_bias)
    lasts = (dgain1, dshift1, dqv_bias)

    def reduce_small(items):
        total = lax.psum(jnp.concatenate(items), ALL)
        outs, at = [], 0
        for item in items:
            size = item.shape[0] // seqs
            outs.append(lax.dynamic_slice_in_dim(total, at + seq_at * size, size))
            at += item.shape[0]
        return outs

    dout_bias, dgain2, dshift2, dfc_bias, dproj_bias = reduce_small(mids)
    dgain1, dshift1, dqv_bias = reduce_small(lasts)
    return (
        hidden_out[None],
        input_grad[None],
        dgain1,
        dshift1,
        dqkv_weight,
        dqv_bias,
        dout_weight,
        dout_bias,
        dgain2,
        dshift2,
        dfc_weight,
        dfc_bias,
        dproj_weight,
        dproj_bias,
    )


def solution(mesh):
    seqs, reps = mesh.shape["seq"], mesh.shape["rep"]
    grid = Mesh(mesh.devices.reshape(4, seqs // 4, reps // 2, 2), ALL)
    wide = P(REP, SEQ, None)
    table = P(REP, None)
    vector = P(SEQ)
    matrix = P(SEQ, None)
    return jax.shard_map(
        shards,
        mesh=grid,
        in_specs=(
            wide,
            wide,
            table,
            table,
            vector,
            vector,
            matrix,
            vector,
            matrix,
            vector,
            vector,
            vector,
            matrix,
            vector,
            matrix,
            vector,
        ),
        out_specs=(
            wide,
            wide,
            vector,
            vector,
            matrix,
            vector,
            matrix,
            vector,
            vector,
            vector,
            matrix,
            vector,
            matrix,
            vector,
        ),
        check_vma=False,
    )
```

```python
import functools
import itertools
import math

import jax
import jax.numpy as jnp
from jax import lax
from jax.experimental import pallas as pl
from jax.experimental.pallas import tpu as pltpu
from jax.sharding import Mesh
from jax.sharding import PartitionSpec as P

HD = 128
EPSILON = 1e-05
NEGATIVE = -1e30
SCALE = 1.0 / math.sqrt(HD)
LOG2E = math.log2(math.e)
GELU_C = math.sqrt(2.0 / math.pi)
SEQ = ("z", "y")
REP = ("x", "c")
PLANE = ("y", "x", "c")
ALL = ("z", "y", "x", "c")
BF16 = jnp.bfloat16
F32 = jnp.float32
HEADS_STEP = 2


def dot(left, right, dims):
    return lax.dot_general(left, right, (dims, ((), ())), preferred_element_type=F32)


NN = ((1,), (0,))
NT = ((1,), (1,))
TN = ((0,), (0,))


def attention_bias(seg_own, seg_ctx, padding_id, rows, ctx):
    t = lax.broadcasted_iota(jnp.int32, (rows, ctx), 0)
    u = lax.broadcasted_iota(jnp.int32, (rows, ctx), 1)
    allowed = (seg_own == seg_ctx) & (u <= t + (ctx - rows)) & (seg_own != padding_id)
    return jnp.where(allowed, 0.0, NEGATIVE).astype(F32)


def forward_kernel(padding_id, q_ref, kv_ref, own_ref, ctx_ref, low_ref, att_ref, norm_ref, bias):
    rows, ctx = bias.shape

    @pl.when(pl.program_id(0) == 0)
    def _():
        bias[...] = attention_bias(own_ref[...], ctx_ref[...], padding_id, rows, ctx)

    live = own_ref[...] != padding_id
    keys = kv_ref[:, :HD]
    values = kv_ref[:, HD:]
    for head in range(HEADS_STEP):
        lanes = slice(head * HD, (head + 1) * HD)
        scores = dot(q_ref[:, lanes], keys, NT) * (SCALE * LOG2E) + bias[...]
        top = jnp.max(scores, axis=1, keepdims=True)
        weights = jnp.exp2(scores - top)
        sums = jnp.sum(weights, axis=1, keepdims=True)
        mixed = dot(weights.astype(BF16), values, NN)
        attended = jnp.where(live, mixed / sums, 0.0)
        att_ref[:, lanes] = attended
        low_ref[:, lanes] = attended.astype(BF16)
        norm = jnp.where(live, top + jnp.log2(sums), 0.0)
        norm_ref[:, lanes] = jnp.broadcast_to(norm, (rows, HD))


def attention_forward(queries, kv_ctx, seg_own, seg_ctx, padding_id):
    rows, width = queries.shape
    ctx = kv_ctx.shape[0]
    step = HEADS_STEP * HD
    tile = pl.BlockSpec((rows, step), lambda h: (0, h))
    return pl.pallas_call(
        functools.partial(forward_kernel, padding_id),
        grid=(width // step,),
        in_specs=[
            tile,
            pl.BlockSpec((ctx, 2 * HD), lambda h: (0, 0)),
            pl.BlockSpec((rows, 1), lambda h: (0, 0)),
            pl.BlockSpec((1, ctx), lambda h: (0, 0)),
        ],
        out_specs=[tile, tile, tile],
        out_shape=[
            jax.ShapeDtypeStruct((rows, width), BF16),
            jax.ShapeDtypeStruct((rows, width), F32),
            jax.ShapeDtypeStruct((rows, width), F32),
        ],
        scratch_shapes=[pltpu.VMEM((rows, ctx), F32)],
        compiler_params=pltpu.CompilerParams(vmem_limit_bytes=40 * 1024 * 1024),
        cost_estimate=pl.CostEstimate(
            flops=4 * rows * ctx * width,
            bytes_accessed=12 * rows * width,
            transcendentals=rows * ctx * width // HD,
        ),
        name="attention_forward",
    )(queries, kv_ctx, seg_own, seg_ctx)


def backward_kernel(
    padding_id, q_ref, g_ref, att_ref, norm_ref, kv_ref, own_ref, ctx_ref, dq_ref, dkv_ref, bias
):
    rows, ctx = bias.shape

    @pl.when(pl.program_id(0) == 0)
    def _():
        bias[...] = attention_bias(own_ref[...], ctx_ref[...], padding_id, rows, ctx)
        dkv_ref[...] = jnp.zeros_like(dkv_ref)

    keys = kv_ref[:, :HD]
    values = kv_ref[:, HD:]
    for head in range(HEADS_STEP):
        lanes = slice(head * HD, (head + 1) * HD)
        q = q_ref[:, lanes]
        g = g_ref[:, lanes]
        delta = jnp.sum(g.astype(F32) * att_ref[:, lanes], axis=1, keepdims=True)
        norm = norm_ref[:, head * HD : head * HD + 1]
        scores = dot(q, keys, NT) * (SCALE * LOG2E) + bias[...]
        prob = jnp.exp2(scores - norm)
        grad_prob = dot(g, values, NT)
        grad_scores = (prob * (grad_prob - delta) * SCALE).astype(BF16)
        dq_ref[:, lanes] = dot(grad_scores, keys, NN).astype(BF16)
        dkv_ref[:, :HD] += dot(grad_scores, q, TN)
        dkv_ref[:, HD:] += dot(prob.astype(BF16), g, TN)


def attention_backward(queries, grads, attended, norms, kv_ctx, seg_own, seg_ctx, padding_id):
    rows, width = queries.shape
    ctx = kv_ctx.shape[0]
    step = HEADS_STEP * HD
    tile = pl.BlockSpec((rows, step), lambda h: (0, h))
    whole = pl.BlockSpec((ctx, 2 * HD), lambda h: (0, 0))
    return pl.pallas_call(
        functools.partial(backward_kernel, padding_id),
        grid=(width // step,),
        in_specs=[
            tile,
            tile,
            tile,
            tile,
            whole,
            pl.BlockSpec((rows, 1), lambda h: (0, 0)),
            pl.BlockSpec((1, ctx), lambda h: (0, 0)),
        ],
        out_specs=[tile, whole],
        out_shape=[
            jax.ShapeDtypeStruct((rows, width), BF16),
            jax.ShapeDtypeStruct((ctx, 2 * HD), F32),
        ],
        scratch_shapes=[pltpu.VMEM((rows, ctx), F32)],
        compiler_params=pltpu.CompilerParams(vmem_limit_bytes=48 * 1024 * 1024),
        cost_estimate=pl.CostEstimate(
            flops=10 * rows * ctx * width,
            bytes_accessed=14 * rows * width,
            transcendentals=rows * ctx * width // HD,
        ),
        name="attention_backward",
    )(queries, grads, attended, norms, kv_ctx, seg_own, seg_ctx)


def norm_parts(values):
    center = values - jnp.mean(values, axis=-1, keepdims=True)
    spread = jnp.mean(center * center, axis=-1, keepdims=True)
    rstd = lax.rsqrt(spread + EPSILON)
    return center * rstd, rstd


def norm_back(grad, unit, rstd, gain):
    scaled = grad * gain
    mean_g = jnp.mean(scaled, axis=-1, keepdims=True)
    mean_gu = jnp.mean(scaled * unit, axis=-1, keepdims=True)
    return rstd * (scaled - mean_g - unit * mean_gu)


def gelu_pair(v):
    inner = jnp.tanh(GELU_C * (v + 0.044715 * v * v * v))
    value = 0.5 * v * (1.0 + inner)
    slope = 0.5 * (1.0 + inner) + 0.5 * v * (1.0 - inner * inner) * GELU_C * (
        1.0 + 3.0 * 0.044715 * v * v
    )
    return value, slope


def swap(block, axis):
    return lax.ppermute(block, axis, [(0, 1), (1, 0)])


def pair(block, axis):
    if lax.axis_size(axis) != 2:
        return lax.all_gather(block, axis, axis=0, tiled=False)
    other = swap(block, axis)
    first = lax.axis_index(axis) == 0
    return jnp.stack([jnp.where(first, block, other), jnp.where(first, other, block)])


def small_plane():
    return lax.axis_size("y") == 2


def plane_pieces(block):
    if not small_plane():
        return [lax.all_gather(block, PLANE, axis=0, tiled=True)]
    half = block.shape[0] // 2
    top, low = block[:half], block[half:]
    top_x, low_y = swap(top, "x"), swap(low, "y")
    top_y, low_x = swap(top, "y"), swap(low, "x")
    top_xy, low_yx = swap(top_x, "y"), swap(low_y, "x")
    near = [top, top_y, top_x, top_xy, low, low_x, low_y, low_yx]
    return near + [swap(item, "c") for item in near]


def gather_plane(block):
    return jnp.concatenate(plane_pieces(block), axis=0)


def scatter_plane(partial, rows, hold=None):
    total = rows * lax.axis_size("y") * lax.axis_size("x") * lax.axis_size("c")
    if not small_plane():
        return lax.psum_scatter(
            partial(0, total).astype(BF16), PLANE, scatter_dimension=0, tiled=True
        ).astype(F32)
    side = total // 2
    got = swap(partial(side, side).astype(BF16), "c")
    both = (partial(0, side) + got.astype(F32)).astype(BF16)
    if hold is not None:
        both, _ = together(both, hold)
    top, low = both[: side // 2], both[side // 2 :]
    got_top, got_low = swap(top[rows:], "x"), swap(low[rows:], "y")
    top = (top[:rows].astype(F32) + got_top.astype(F32)).astype(BF16)
    low = (low[:rows].astype(F32) + got_low.astype(F32)).astype(BF16)
    half = rows // 2
    got_top, got_low = swap(top[half:], "y"), swap(low[half:], "x")
    return jnp.concatenate(
        [
            top[:half].astype(F32) + got_top.astype(F32),
            low[:half].astype(F32) + got_low.astype(F32),
        ],
        axis=0,
    )


def shift(block, axis, by):
    count = math.prod(lax.axis_size(a) for a in ([axis] if isinstance(axis, str) else axis))
    return lax.ppermute(block, axis, [(i, (i + by) % count) for i in range(count)])


def place_kernel(count, parts, offsets, *refs):
    out = refs[count]
    for i in range(count):
        rows = refs[i].shape[0] // parts
        for j in range(parts):
            start = pl.multiple_of(offsets[i * parts + j], rows)
            out[pl.ds(start, rows), :] = refs[i][j * rows : (j + 1) * rows, :]


def place_rows(pieces, parts, offsets):
    count = len(pieces)
    rows, width = pieces[0].shape
    return pl.pallas_call(
        functools.partial(place_kernel, count, parts),
        grid_spec=pltpu.PrefetchScalarGridSpec(
            num_scalar_prefetch=1,
            grid=(1,),
            in_specs=[pl.BlockSpec((rows, width), lambda i, at: (0, 0))] * count,
            out_specs=pl.BlockSpec((count * rows, width), lambda i, at: (0, 0)),
        ),
        out_shape=jax.ShapeDtypeStruct((count * rows, width), pieces[0].dtype),
        compiler_params=pltpu.CompilerParams(vmem_limit_bytes=56 * 1024 * 1024),
        cost_estimate=pl.CostEstimate(
            flops=0, bytes_accessed=4 * count * rows * width, transcendentals=0
        ),
        name="place_rows",
    )(offsets, *pieces)


def assemble_kernel(count, slices, by_column, rolled, offsets, *refs):
    outs = refs[count:]
    if rolled is not None:
        total = jnp.zeros((refs[0].shape[0], 2 * HD), F32)
    for i in range(count):
        for row, rows, first, cols, target, base in slices:
            values = refs[i][row : row + rows, first : first + cols].astype(F32)
            if by_column:
                start = pl.multiple_of(offsets[i] + base, HD)
                outs[target][:, pl.ds(start, cols)] = values
            else:
                start = pl.multiple_of(offsets[i], rows)
                outs[target][pl.ds(start, rows), base : base + cols] = values
        if rolled is not None:
            first, wide, target, at = rolled
            narrow = refs[i][:, first : first + wide].astype(F32)
            padded = jnp.concatenate(
                [narrow, jnp.zeros((narrow.shape[0], 2 * HD - wide), F32)], axis=1
            )
            total = total + pltpu.roll(padded, offsets[i] * wide // slices[0][3], 1)
    if rolled is not None:
        outs[target][:, at : at + 2 * HD] = total


def assemble(pieces, slices, shapes, offsets, by_column=False, rolled=None):
    count = len(pieces)
    rows, width = pieces[0].shape
    return pl.pallas_call(
        functools.partial(assemble_kernel, count, slices, by_column, rolled),
        grid_spec=pltpu.PrefetchScalarGridSpec(
            num_scalar_prefetch=1,
            grid=(1,),
            in_specs=[pl.BlockSpec((rows, width), lambda i, at: (0, 0))] * count,
            out_specs=[pl.BlockSpec(shape, lambda i, at: (0, 0)) for shape in shapes],
        ),
        out_shape=[jax.ShapeDtypeStruct(shape, F32) for shape in shapes],
        compiler_params=pltpu.CompilerParams(vmem_limit_bytes=56 * 1024 * 1024),
        cost_estimate=pl.CostEstimate(
            flops=0, bytes_accessed=6 * count * rows * width, transcendentals=0
        ),
        name="assemble_rows",
    )(offsets, *pieces)


def together(*values):
    return lax.optimization_barrier(values)


def spread_near(column):
    side = column.shape[0] // 2
    near = []
    for part in range(2):
        own = column[part * side : (part + 1) * side]
        one, two = ("x", "y") if part == 0 else ("y", "x")
        near += [own, swap(own, one), swap(own, two)]
    return near


def spread_far(near):
    zs = lax.axis_size("z")
    y, x, c = (lax.axis_index(a) for a in PLANE)
    rows = near[0].shape[0] // (zs // 2)
    pieces, offsets = [], []
    for part in range(2):
        one, two = ("x", "y") if part == 0 else ("y", "x")
        own, by_one, by_two = near[3 * part : 3 * part + 3]
        for item, at_one, at_two in (
            (own, 0, 0),
            (by_one, 1, 0),
            (by_two, 0, 1),
            (swap(by_one, two), 1, 1),
        ):
            dx, dy = (at_one, at_two) if one == "x" else (at_two, at_one)
            for dc in range(2):
                pieces.append(swap(item, "c") if dc else item)
                source = ((y ^ dy) * 2 + (x ^ dx)) * 2 + (c ^ dc)
                for z in range(zs // 2):
                    offsets.append(((part * (zs // 2) + z) * 8 + source) * rows)
    return place_rows(pieces, zs // 2, jnp.stack(offsets).astype(jnp.int32))


def shards(
    hidden_in,
    out_grad,
    segment_ids,
    row_position,
    gain_first,
    shift_first,
    qkv_weight,
    qv_bias,
    out_weight,
    out_bias,
    gain_second,
    shift_second,
    fc_weight,
    fc_bias,
    proj_weight,
    proj_bias,
):
    zs, ys, xs, cs = (lax.axis_size(a) for a in ALL)
    reps = xs * cs
    plane = ys * reps
    seqs = zs * ys
    z_at, y_at, x_at, c_at = (lax.axis_index(a) for a in ALL)
    q_at = x_at * cs + c_at
    f_at = y_at * reps + q_at
    seq_at = z_at * ys + y_at
    rows = hidden_in.shape[1]
    width = hidden_in.shape[2]
    window = rows * seqs
    capacity = 2 * rows // seqs
    halo = max(1, seqs // 4)
    ctx = (halo + 1) * rows
    padding_id = max(8, window // 256) - 1
    qkv_cols = qkv_weight.shape[1]
    ff = fc_weight.shape[1]
    ff_unit = ff // seqs // reps
    ff_own = zs * ff_unit
    shard = width // seqs

    def fc_columns(y):
        picked = []
        for z in range(zs):
            start = ((z * ys + y) * reps + q_at) * ff_unit
            picked.append(lax.dynamic_slice_in_dim(fc_weight, start, ff_unit, 1))
        return jnp.concatenate(picked, axis=1)

    if ys == 2:
        fc_mine, fc_other = fc_columns(y_at), swap(fc_columns(1 - y_at), "y")
        fc_pair = jnp.concatenate(
            [jnp.where(y_at == 0, fc_mine, fc_other), jnp.where(y_at == 0, fc_other, fc_mine)]
        )
    else:
        fc_pair = lax.all_to_all(
            jnp.stack([fc_columns(y) for y in range(ys)]), "y", 0, 0, tiled=True
        ).reshape(ys * shard, ff_own)

    places = row_position[0]
    segments = segment_ids[0]
    targets = (places // rows).reshape(seqs, rows)
    earlier = (
        lax.broadcasted_iota(jnp.int32, (rows, rows), 1)
        < lax.broadcasted_iota(jnp.int32, (rows, rows), 0)
    )
    same = (targets[:, :, None] == targets[:, None, :]) & earlier[None]
    ranks = jnp.sum(same.astype(jnp.int32), axis=2).reshape(window)
    first_row = seq_at * rows
    slots = seqs * capacity
    send_slots = lax.dynamic_slice_in_dim(places // rows * capacity + ranks, first_row, rows)
    arrive_slots = jnp.arange(window, dtype=jnp.int32) // rows * capacity + ranks
    own_places = first_row + jnp.arange(rows, dtype=jnp.int32)
    recv_slots = jnp.sum(
        jnp.where(places[None, :] == own_places[:, None], arrive_slots[None, :], 0), axis=1
    )
    slot_ids = jnp.arange(slots, dtype=jnp.int32)
    pick_send = (send_slots[:, None] == slot_ids[None, :]).astype(BF16)
    pick_recv = (recv_slots[:, None] == slot_ids[None, :]).astype(BF16)

    def exchange_first(values):
        wide = capacity + extra
        wide_ids = jnp.arange(seqs * wide, dtype=jnp.int32)
        send_wide = send_slots // capacity * wide + send_slots % capacity
        recv_wide = recv_slots // capacity * wide + recv_slots % capacity
        pick_rows = (send_wide[:, None] == wide_ids[None, :]).astype(BF16)
        pick_small = (wide_ids % wide - capacity)[None, :] == jnp.arange(extra)[:, None]
        packed = dot(
            jnp.concatenate([pick_rows, pick_small.astype(BF16)], axis=0),
            jnp.concatenate([values, small_rows], axis=0),
            TN,
        )
        packed = packed.astype(BF16).reshape(seqs, wide, width)
        moved = lax.all_to_all(packed, SEQ, split_axis=0, concat_axis=0, tiled=True)
        return moved, recv_wide, wide_ids

    def arrive_first(moved, recv_wide, wide_ids):
        pick_wide = (recv_wide[:, None] == wide_ids[None, :]).astype(BF16)
        every = moved[:, capacity:].reshape(seqs, extra * width)[:, : small.shape[0]]
        return dot(pick_wide, moved.reshape(wide_ids.shape[0], width), NN), every.astype(F32)

    def exchange(values, pick_out, pick_in):
        packed = dot(pick_out, values, TN).astype(BF16).reshape(seqs, capacity, values.shape[1])
        moved = lax.all_to_all(packed, SEQ, split_axis=0, concat_axis=0, tiled=True)
        return dot(pick_in, moved.reshape(slots, values.shape[1]), NN)

    def to_places(values):
        return exchange(values, pick_send, pick_recv)

    def to_stored(values):
        return exchange(values, pick_recv, pick_send)

    vectors = (
        gain_first,
        shift_first,
        qv_bias,
        out_bias,
        gain_second,
        shift_second,
        fc_bias,
        proj_bias,
    )
    small = jnp.concatenate(vectors)
    extra = -(-small.shape[0] // (8 * width)) * 8
    small_rows = jnp.pad(small, (0, extra * width - small.shape[0])).reshape(extra, width)

    def quarter(weight):
        size = weight.shape[0] // reps
        return lax.dynamic_slice_in_dim(weight, q_at * size, size, 0)

    proj_rows = quarter(proj_weight)
    parts = [slice(p * ff_own, (p + 1) * ff_own) for p in range(width // ff_own)]
    fc_rows = ys * shard
    units_part = jnp.concatenate([fc_pair] + [proj_rows[:, part] for part in parts], axis=0)
    with jax.named_scope("attention_weights"):
        if small_plane():
            columns = lax.all_gather(
                jnp.concatenate([quarter(qkv_weight), quarter(out_weight)], axis=1),
                "z",
                axis=0,
                tiled=True,
            )
        else:
            columns = lax.all_gather(quarter(qkv_weight), ALL, axis=0, tiled=True)
    with jax.named_scope("hidden_to_places"):
        moved, *picks = exchange_first(hidden_in[0])
    units_part, grad_stored, columns, moved = together(
        units_part, out_grad[0], columns, moved
    )
    with jax.named_scope("units_gather"):
        hidden_units = lax.all_gather(units_part, "z", axis=0, tiled=False)

    with jax.named_scope("hidden_to_places"):
        inputs, small_all = arrive_first(moved, *picks)
    if small_plane():
        qkv_near = spread_near(columns[:, :qkv_cols])
        out_column, *qkv_near = together(columns[:, qkv_cols:], *qkv_near)
        with jax.named_scope("qkv_gather"):
            full_qkv = spread_far(qkv_near)
        with jax.named_scope("out_gather"):
            full_out = spread_far(spread_near(out_column))
    else:
        full_qkv = columns
        full_out = lax.all_gather(quarter(out_weight), ALL, axis=0, tiled=True)
    wholes = []
    at = 0
    for item in vectors:
        wholes.append(small_all[:, at : at + item.shape[0]].reshape(-1))
        at += item.shape[0]
    gain1, shift1, qv_full, out_shift, gain2, shift2, fc_shift, proj_shift = wholes
    fc_shift_own = lax.dynamic_slice(
        fc_shift.reshape(zs, ys, reps, ff_unit), (0, y_at, q_at, 0), (zs, 1, 1, ff_unit)
    ).reshape(ff_own)

    unit1, rstd1 = norm_parts(inputs)
    normed1 = (unit1 * gain1 + shift1).astype(BF16)
    projected = dot(normed1, full_qkv, NN)
    queries = (projected[:, :width] + qv_full[:width]).astype(BF16)
    kv_shift = jnp.concatenate([jnp.zeros((HD,), F32), qv_full[width:]])
    kv_own = (projected[:, width:] + kv_shift).astype(BF16)
    blocks = []
    for back in range(halo, 0, -1):
        pairs = [(i, i + back) for i in range(seqs - back)]
        blocks.append(lax.ppermute(kv_own, SEQ, pairs))
    kv_ctx = jnp.concatenate(blocks + [kv_own], axis=0)
    seg_own = lax.dynamic_slice_in_dim(segments, first_row, rows)[:, None]
    seg_padded = jnp.concatenate([jnp.full((halo * rows,), -1, jnp.int32), segments])
    seg_ctx = lax.dynamic_slice_in_dim(seg_padded, first_row, ctx)[None, :]
    attended_low, attended, norms = attention_forward(
        queries, kv_ctx, seg_own, seg_ctx, padding_id
    )
    with jax.named_scope("grad_to_places"):
        grad_f32 = to_places(grad_stored)
    attended_low, grad_f32 = together(attended_low, grad_f32)
    grad_low = grad_f32.astype(BF16)
    with jax.named_scope("grad_gather"):
        grad_all = gather_plane(grad_low)
    middle = inputs + (dot(attended_low, full_out, NN) + out_shift)

    unit2, rstd2 = norm_parts(middle)
    normed2 = (unit2 * gain2 + shift2).astype(BF16)
    with jax.named_scope("normed2_gather"):
        normed2_all = gather_plane(normed2)
    with jax.named_scope("both_gather"):
        both_low, normed2_all = together(
            jnp.concatenate([normed1, attended_low], axis=1), normed2_all
        )
        both_all = lax.all_gather(both_low, PLANE, axis=0, tiled=True)
    fc_own = hidden_units[:, :fc_rows].reshape(width, ff_own)
    proj_parts = [
        hidden_units[:, fc_rows + p * ff_unit : fc_rows + (p + 1) * ff_unit].reshape(ff_own, ff_own)
        for p in range(len(parts))
    ]

    pre_act = dot(normed2_all, fc_own, NN) + fc_shift_own
    act, slope = gelu_pair(pre_act)
    act_low = act.astype(BF16)
    grad_act = sum(dot(grad_all[:, part], own, NT) for part, own in zip(parts, proj_parts))
    grad_pre = (grad_act * slope).astype(BF16)
    dfc_bias_own = jnp.sum(grad_pre.astype(F32), axis=0)

    def over_z(partial):
        return lax.psum_scatter(partial, "z", scatter_dimension=0, tiled=True)

    unit_terms = [dot(normed2_all, grad_pre, TN).reshape(zs, fc_rows, ff_own)]
    for part in parts:
        unit_terms.append(dot(act_low, grad_all[:, part], TN).reshape(zs, ff_unit, ff_own))
    unit_terms = jnp.concatenate(unit_terms, axis=1).astype(BF16).reshape(-1, ff_own)
    unit_terms, both_all = together(unit_terms, both_all)
    normed1_all, attended_all = both_all[:, :width], both_all[:, width:]
    with jax.named_scope("grad_normed2_scatter"):
        grad_normed2 = scatter_plane(
            lambda first, count: dot(grad_pre[first : first + count], fc_own, NT),
            rows,
            unit_terms,
        )
    units = over_z(unit_terms)
    dgain2 = jnp.sum(grad_normed2 * unit2, axis=0)
    dshift2 = jnp.sum(grad_normed2, axis=0)
    dproj_bias = jnp.sum(grad_f32, axis=0)
    grad_middle = grad_f32 + norm_back(grad_normed2, unit2, rstd2, gain2)

    grad_branch = grad_middle.astype(BF16)
    dout_bias = jnp.sum(grad_branch.astype(F32), axis=0)
    grad_attended = dot(grad_branch, full_out, NT).astype(BF16)
    dq, dkv_ctx = attention_backward(
        queries, grad_attended, attended, norms, kv_ctx, seg_own, seg_ctx, padding_id
    )
    act_late, dq = together(act_low, dq)
    with jax.named_scope("mlp_out_scatter"):
        mlp_out = scatter_plane(
            lambda first, count: jnp.concatenate(
                [dot(act_late[first : first + count], own, NN) for own in proj_parts], axis=1
            ),
            rows,
        )
    result = (middle + mlp_out + proj_shift).astype(BF16)
    with jax.named_scope("result_to_stored"):
        hidden_out = to_stored(result).astype(BF16)
    dkv = dkv_ctx[halo * rows :]
    for back in range(1, halo + 1):
        pairs = [(i + back, i) for i in range(seqs - back)]
        term = dkv_ctx[(halo - back) * rows : (halo - back + 1) * rows].astype(BF16)
        dkv = dkv + lax.ppermute(term, SEQ, pairs).astype(F32)
    grad_qkv = jnp.concatenate([dq, dkv.astype(BF16)], axis=1)
    grad_normed1 = dot(grad_qkv, full_qkv, NT)
    dgain1 = jnp.sum(grad_normed1 * unit1, axis=0)
    dshift1 = jnp.sum(grad_normed1, axis=0)
    grad_in = grad_middle + norm_back(grad_normed1, unit1, rstd1, gain1)
    with jax.named_scope("input_grad_to_stored"):
        input_grad = to_stored(grad_in.astype(BF16))
    grad_qkv_f32 = grad_qkv.astype(F32)
    dqv_bias = jnp.concatenate(
        [jnp.sum(grad_qkv_f32[:, :width], axis=0), jnp.sum(grad_qkv_f32[:, width + HD :], axis=0)]
    )

    def columns_of_plane(values):
        parts = [values[:, :width].reshape(rows, plane, width // plane)]
        if values.shape[1] > width:
            parts.append(values[:, width:].reshape(rows, plane, -1))
        sent = jnp.concatenate(parts, axis=2).transpose(1, 0, 2)
        cols = sent.shape[2]
        return lax.all_to_all(sent, PLANE, split_axis=0, concat_axis=0, tiled=True).reshape(
            plane * rows, cols
        )

    dout_own = dot(attended_all, columns_of_plane(grad_branch), TN).astype(BF16)
    dqkv_own = dot(normed1_all, columns_of_plane(grad_qkv), TN).astype(BF16)

    first_row_y = y_at * shard
    flipped = (1 - y_at) * shard

    def rows_of_y(partial):
        cols = partial.shape[1]
        if ys == 2:
            kept = lax.dynamic_slice_in_dim(partial, first_row_y, shard, 0)
            return [kept, swap(lax.dynamic_slice_in_dim(partial, flipped, shard, 0), "y")]
        moved = lax.all_to_all(
            partial.reshape(ys, shard, cols), "y", split_axis=0, concat_axis=0, tiled=True
        )
        return [moved[y] for y in range(ys)]

    def near_rep(pieces):
        return pieces + [swap(item, "x") for item in pieces]

    def far_rep(pieces):
        return pieces + [swap(item, "c") for item in pieces]

    def sources(count):
        found = []
        for dc, dx, dy in itertools.product(range(2), range(2), range(count)):
            y = (y_at ^ dy) if ys == 2 else dy
            found.append((y * reps if count > 1 else 0) + (x_at ^ dx) * cs + (c_at ^ dc))
        return jnp.stack(found).astype(jnp.int32)

    proj_near = near_rep([units[fc_rows:]])
    fc_near = near_rep(rows_of_y(units[:fc_rows]))
    head_terms, input_grad, hidden_out, proj_near, fc_near = together(
        jnp.concatenate([dqkv_own, dout_own], axis=1), input_grad, hidden_out, proj_near, fc_near
    )
    with jax.named_scope("proj_grad_rows"):
        proj_pieces = far_rep(proj_near)
        dproj_weight = assemble(
            proj_pieces,
            [(p * ff_unit, ff_unit, 0, ff_own, 0, p * ff_own) for p in range(len(parts))],
            [(ff // seqs, width)],
            sources(1) * ff_unit,
        )[0]
    with jax.named_scope("fc_grad_rows"):
        fc_pieces = far_rep(fc_near)
        if small_plane():
            dfc_weight = assemble(
                fc_pieces,
                [(0, shard, z * ff_unit, ff_unit, 0, z * plane * ff_unit) for z in range(zs)],
                [(shard, ff)],
                sources(ys) * ff_unit,
                by_column=True,
            )[0]
        else:
            stacked = jnp.stack(fc_pieces).reshape(plane, shard, zs, ff_unit)
            order = jnp.argsort(sources(ys))
            dfc_weight = (
                stacked[order].transpose(1, 2, 0, 3).reshape(shard, ff).astype(F32)
            )
    with jax.named_scope("attention_grad_rows"):
        heads = over_z(head_terms)
        head_pieces = far_rep(near_rep(rows_of_y(heads)))
        q_cols, kv_cols = width // plane, 2 * HD // plane
        if small_plane():
            dqkv_weight, dout_weight = assemble(
                head_pieces,
                [(0, shard, 0, q_cols, 0, 0), (0, shard, q_cols + kv_cols, q_cols, 1, 0)],
                [(shard, qkv_cols), (shard, width)],
                sources(ys) * q_cols,
                by_column=True,
                rolled=(q_cols, kv_cols, 0, width),
            )
        else:
            stacked = jnp.stack(head_pieces)[jnp.argsort(sources(ys))].transpose(1, 0, 2)
            stacked = stacked.astype(F32)
            dq_cols = stacked[:, :, :q_cols].reshape(shard, width)
            dkv_cols = stacked[:, :, q_cols : q_cols + kv_cols].reshape(shard, 2 * HD)
            dqkv_weight = jnp.concatenate([dq_cols, dkv_cols], axis=1)
            dout_weight = stacked[:, :, q_cols + kv_cols :].reshape(shard, width)

    dfc_bias = lax.dynamic_update_slice(
        jnp.zeros((zs, ys, reps, ff_unit), F32),
        dfc_bias_own.reshape(zs, 1, 1, ff_unit),
        (0, y_at, q_at, 0),
    ).reshape(ff)
    mids = (dout_bias, dgain2, dshift2, dfc_bias, dproj_bias)
    lasts = (dgain1, dshift1, dqv_bias)

    def reduce_small(items):
        total = jnp.concatenate(items).reshape(-1, HD)
        if small_plane():
            for axis in ("c", "x", "y"):
                total = total + swap(total, axis)
            total = sum([shift(total, "z", away) for away in range(1, zs)], total)
        else:
            total = lax.psum(total, ALL)
        total = total.reshape(-1)
        outs, at = [], 0
        for item in items:
            size = item.shape[0] // seqs
            outs.append(lax.dynamic_slice_in_dim(total, at + seq_at * size, size))
            at += item.shape[0]
        return outs

    dout_bias, dgain2, dshift2, dfc_bias, dproj_bias = reduce_small(mids)
    dgain1, dshift1, dqv_bias = reduce_small(lasts)
    return (
        hidden_out[None],
        input_grad[None],
        dgain1,
        dshift1,
        dqkv_weight,
        dqv_bias,
        dout_weight,
        dout_bias,
        dgain2,
        dshift2,
        dfc_weight,
        dfc_bias,
        dproj_weight,
        dproj_bias,
    )


def solution(mesh):
    seqs, reps = mesh.shape["seq"], mesh.shape["rep"]
    grid = Mesh(mesh.devices.reshape(4, seqs // 4, reps // 2, 2), ALL)
    wide = P(REP, SEQ, None)
    table = P(REP, None)
    vector = P(SEQ)
    matrix = P(SEQ, None)
    return jax.shard_map(
        shards,
        mesh=grid,
        in_specs=(
            wide,
            wide,
            table,
            table,
            vector,
            vector,
            matrix,
            vector,
            matrix,
            vector,
            vector,
            vector,
            matrix,
            vector,
            matrix,
            vector,
        ),
        out_specs=(
            wide,
            wide,
            vector,
            vector,
            matrix,
            vector,
            matrix,
            vector,
            vector,
            vector,
            matrix,
            vector,
            matrix,
            vector,
        ),
        check_vma=False,
    )
```

```python
import functools
import itertools
import math

import jax
import jax.numpy as jnp
from jax import lax
from jax.experimental import pallas as pl
from jax.experimental.pallas import tpu as pltpu
from jax.sharding import Mesh
from jax.sharding import PartitionSpec as P

HD = 128
EPSILON = 1e-05
NEGATIVE = -1e30
SCALE = 1.0 / math.sqrt(HD)
LOG2E = math.log2(math.e)
GELU_C = math.sqrt(2.0 / math.pi)
SEQ = ("z", "y")
REP = ("x", "c")
PLANE = ("y", "x", "c")
ALL = ("z", "y", "x", "c")
BF16 = jnp.bfloat16
F32 = jnp.float32
HEADS_STEP = 2


def dot(left, right, dims):
    return lax.dot_general(left, right, (dims, ((), ())), preferred_element_type=F32)


NN = ((1,), (0,))
NT = ((1,), (1,))
TN = ((0,), (0,))


def attention_bias(seg_own, seg_ctx, padding_id, rows, ctx):
    t = lax.broadcasted_iota(jnp.int32, (rows, ctx), 0)
    u = lax.broadcasted_iota(jnp.int32, (rows, ctx), 1)
    allowed = (seg_own == seg_ctx) & (u <= t + (ctx - rows)) & (seg_own != padding_id)
    return jnp.where(allowed, 0.0, NEGATIVE).astype(F32)


def forward_kernel(padding_id, q_ref, kv_ref, own_ref, ctx_ref, low_ref, att_ref, norm_ref, bias):
    rows, ctx = bias.shape

    @pl.when(pl.program_id(0) == 0)
    def _():
        bias[...] = attention_bias(own_ref[...], ctx_ref[...], padding_id, rows, ctx)

    live = own_ref[...] != padding_id
    keys = kv_ref[:, :HD]
    values = kv_ref[:, HD:]
    for head in range(HEADS_STEP):
        lanes = slice(head * HD, (head + 1) * HD)
        scores = dot(q_ref[:, lanes], keys, NT) * (SCALE * LOG2E) + bias[...]
        top = jnp.max(scores, axis=1, keepdims=True)
        weights = jnp.exp2(scores - top)
        sums = jnp.sum(weights, axis=1, keepdims=True)
        mixed = dot(weights.astype(BF16), values, NN)
        attended = jnp.where(live, mixed / sums, 0.0)
        att_ref[:, lanes] = attended
        low_ref[:, lanes] = attended.astype(BF16)
        norm = jnp.where(live, top + jnp.log2(sums), 0.0)
        norm_ref[:, lanes] = jnp.broadcast_to(norm, (rows, HD))


def attention_forward(queries, kv_ctx, seg_own, seg_ctx, padding_id):
    rows, width = queries.shape
    ctx = kv_ctx.shape[0]
    step = HEADS_STEP * HD
    tile = pl.BlockSpec((rows, step), lambda h: (0, h))
    return pl.pallas_call(
        functools.partial(forward_kernel, padding_id),
        grid=(width // step,),
        in_specs=[
            tile,
            pl.BlockSpec((ctx, 2 * HD), lambda h: (0, 0)),
            pl.BlockSpec((rows, 1), lambda h: (0, 0)),
            pl.BlockSpec((1, ctx), lambda h: (0, 0)),
        ],
        out_specs=[tile, tile, tile],
        out_shape=[
            jax.ShapeDtypeStruct((rows, width), BF16),
            jax.ShapeDtypeStruct((rows, width), F32),
            jax.ShapeDtypeStruct((rows, width), F32),
        ],
        scratch_shapes=[pltpu.VMEM((rows, ctx), F32)],
        compiler_params=pltpu.CompilerParams(vmem_limit_bytes=40 * 1024 * 1024),
        cost_estimate=pl.CostEstimate(
            flops=4 * rows * ctx * width,
            bytes_accessed=12 * rows * width,
            transcendentals=rows * ctx * width // HD,
        ),
        name="attention_forward",
    )(queries, kv_ctx, seg_own, seg_ctx)


def backward_kernel(
    padding_id, q_ref, g_ref, att_ref, norm_ref, kv_ref, own_ref, ctx_ref, dq_ref, dkv_ref, bias
):
    rows, ctx = bias.shape

    @pl.when(pl.program_id(0) == 0)
    def _():
        bias[...] = attention_bias(own_ref[...], ctx_ref[...], padding_id, rows, ctx)
        dkv_ref[...] = jnp.zeros_like(dkv_ref)

    keys = kv_ref[:, :HD]
    values = kv_ref[:, HD:]
    for head in range(HEADS_STEP):
        lanes = slice(head * HD, (head + 1) * HD)
        q = q_ref[:, lanes]
        g = g_ref[:, lanes]
        delta = jnp.sum(g.astype(F32) * att_ref[:, lanes], axis=1, keepdims=True)
        norm = norm_ref[:, head * HD : head * HD + 1]
        scores = dot(q, keys, NT) * (SCALE * LOG2E) + bias[...]
        prob = jnp.exp2(scores - norm)
        grad_prob = dot(g, values, NT)
        grad_scores = (prob * (grad_prob - delta) * SCALE).astype(BF16)
        dq_ref[:, lanes] = dot(grad_scores, keys, NN).astype(BF16)
        dkv_ref[:, :HD] += dot(grad_scores, q, TN)
        dkv_ref[:, HD:] += dot(prob.astype(BF16), g, TN)


def attention_backward(queries, grads, attended, norms, kv_ctx, seg_own, seg_ctx, padding_id):
    rows, width = queries.shape
    ctx = kv_ctx.shape[0]
    step = HEADS_STEP * HD
    tile = pl.BlockSpec((rows, step), lambda h: (0, h))
    whole = pl.BlockSpec((ctx, 2 * HD), lambda h: (0, 0))
    return pl.pallas_call(
        functools.partial(backward_kernel, padding_id),
        grid=(width // step,),
        in_specs=[
            tile,
            tile,
            tile,
            tile,
            whole,
            pl.BlockSpec((rows, 1), lambda h: (0, 0)),
            pl.BlockSpec((1, ctx), lambda h: (0, 0)),
        ],
        out_specs=[tile, whole],
        out_shape=[
            jax.ShapeDtypeStruct((rows, width), BF16),
            jax.ShapeDtypeStruct((ctx, 2 * HD), F32),
        ],
        scratch_shapes=[pltpu.VMEM((rows, ctx), F32)],
        compiler_params=pltpu.CompilerParams(vmem_limit_bytes=48 * 1024 * 1024),
        cost_estimate=pl.CostEstimate(
            flops=10 * rows * ctx * width,
            bytes_accessed=14 * rows * width,
            transcendentals=rows * ctx * width // HD,
        ),
        name="attention_backward",
    )(queries, grads, attended, norms, kv_ctx, seg_own, seg_ctx)


def norm_parts(values):
    center = values - jnp.mean(values, axis=-1, keepdims=True)
    spread = jnp.mean(center * center, axis=-1, keepdims=True)
    rstd = lax.rsqrt(spread + EPSILON)
    return center * rstd, rstd


def norm_back(grad, unit, rstd, gain):
    scaled = grad * gain
    mean_g = jnp.mean(scaled, axis=-1, keepdims=True)
    mean_gu = jnp.mean(scaled * unit, axis=-1, keepdims=True)
    return rstd * (scaled - mean_g - unit * mean_gu)


def gelu_pair(v):
    inner = jnp.tanh(GELU_C * (v + 0.044715 * v * v * v))
    value = 0.5 * v * (1.0 + inner)
    slope = 0.5 * (1.0 + inner) + 0.5 * v * (1.0 - inner * inner) * GELU_C * (
        1.0 + 3.0 * 0.044715 * v * v
    )
    return value, slope


def swap(block, axis):
    return lax.ppermute(block, axis, [(0, 1), (1, 0)])


def pair(block, axis):
    if lax.axis_size(axis) != 2:
        return lax.all_gather(block, axis, axis=0, tiled=False)
    other = swap(block, axis)
    first = lax.axis_index(axis) == 0
    return jnp.stack([jnp.where(first, block, other), jnp.where(first, other, block)])


def small_plane():
    return lax.axis_size("y") == 2


def plane_pieces(block):
    if not small_plane():
        return [lax.all_gather(block, PLANE, axis=0, tiled=True)]
    half = block.shape[0] // 2
    top, low = block[:half], block[half:]
    top_x, low_y = swap(top, "x"), swap(low, "y")
    top_y, low_x = swap(top, "y"), swap(low, "x")
    top_xy, low_yx = swap(top_x, "y"), swap(low_y, "x")
    near = [top, top_y, top_x, top_xy, low, low_x, low_y, low_yx]
    return near + [swap(item, "c") for item in near]


def join_kernel(count, *refs):
    rows = refs[0].shape[0]
    for i in range(count):
        refs[count][i * rows : (i + 1) * rows, :] = refs[i][...]


def join_rows(pieces):
    count = len(pieces)
    if count == 1:
        return pieces[0]
    rows, width = pieces[0].shape
    return pl.pallas_call(
        functools.partial(join_kernel, count),
        grid=(1,),
        in_specs=[pl.BlockSpec((rows, width), lambda i: (0, 0))] * count,
        out_specs=pl.BlockSpec((count * rows, width), lambda i: (0, 0)),
        out_shape=jax.ShapeDtypeStruct((count * rows, width), pieces[0].dtype),
        compiler_params=pltpu.CompilerParams(vmem_limit_bytes=56 * 1024 * 1024),
        cost_estimate=pl.CostEstimate(
            flops=0, bytes_accessed=4 * count * rows * width, transcendentals=0
        ),
        name="join_rows",
    )(*pieces)


def gather_plane(block):
    return join_rows(plane_pieces(block))


def scatter_plane(partial, rows, hold=None):
    total = rows * lax.axis_size("y") * lax.axis_size("x") * lax.axis_size("c")
    if not small_plane():
        return lax.psum_scatter(
            partial(0, total).astype(BF16), PLANE, scatter_dimension=0, tiled=True
        ).astype(F32), hold
    side = total // 2
    got = swap(partial(side, side).astype(BF16), "c")
    both = (partial(0, side) + got.astype(F32)).astype(BF16)
    if hold is not None:
        both, _ = together(both, hold)
    top, low = both[: side // 2], both[side // 2 :]
    got_top, got_low = swap(top[rows:], "x"), swap(low[rows:], "y")
    top = (top[:rows].astype(F32) + got_top.astype(F32)).astype(BF16)
    low = (low[:rows].astype(F32) + got_low.astype(F32)).astype(BF16)
    half = rows // 2
    got_top, got_low = swap(top[half:], "y"), swap(low[half:], "x")
    sums = jnp.concatenate(
        [
            top[:half].astype(F32) + got_top.astype(F32),
            low[:half].astype(F32) + got_low.astype(F32),
        ],
        axis=0,
    )
    return sums, got_low


def shift(block, axis, by):
    count = math.prod(lax.axis_size(a) for a in ([axis] if isinstance(axis, str) else axis))
    return lax.ppermute(block, axis, [(i, (i + by) % count) for i in range(count)])


def place_kernel(count, parts, offsets, *refs):
    out = refs[count]
    for i in range(count):
        rows = refs[i].shape[0] // parts
        for j in range(parts):
            start = pl.multiple_of(offsets[i * parts + j], rows)
            out[pl.ds(start, rows), :] = refs[i][j * rows : (j + 1) * rows, :]


def place_rows(pieces, parts, offsets):
    count = len(pieces)
    rows, width = pieces[0].shape
    return pl.pallas_call(
        functools.partial(place_kernel, count, parts),
        grid_spec=pltpu.PrefetchScalarGridSpec(
            num_scalar_prefetch=1,
            grid=(1,),
            in_specs=[pl.BlockSpec((rows, width), lambda i, at: (0, 0))] * count,
            out_specs=pl.BlockSpec((count * rows, width), lambda i, at: (0, 0)),
        ),
        out_shape=jax.ShapeDtypeStruct((count * rows, width), pieces[0].dtype),
        compiler_params=pltpu.CompilerParams(vmem_limit_bytes=56 * 1024 * 1024),
        cost_estimate=pl.CostEstimate(
            flops=0, bytes_accessed=4 * count * rows * width, transcendentals=0
        ),
        name="place_rows",
    )(offsets, *pieces)


def assemble_kernel(count, slices, by_column, rolled, offsets, *refs):
    outs = refs[count:]
    if rolled is not None:
        total = jnp.zeros((refs[0].shape[0], 2 * HD), F32)
    for i in range(count):
        for row, rows, first, cols, target, base in slices:
            values = refs[i][row : row + rows, first : first + cols].astype(F32)
            if by_column:
                start = pl.multiple_of(offsets[i] + base, HD)
                outs[target][:, pl.ds(start, cols)] = values
            else:
                start = pl.multiple_of(offsets[i], rows)
                outs[target][pl.ds(start, rows), base : base + cols] = values
        if rolled is not None:
            first, wide, target, at = rolled
            narrow = refs[i][:, first : first + wide].astype(F32)
            padded = jnp.concatenate(
                [narrow, jnp.zeros((narrow.shape[0], 2 * HD - wide), F32)], axis=1
            )
            total = total + pltpu.roll(padded, offsets[i] * wide // slices[0][3], 1)
    if rolled is not None:
        outs[target][:, at : at + 2 * HD] = total


def assemble(pieces, slices, shapes, offsets, by_column=False, rolled=None):
    count = len(pieces)
    rows, width = pieces[0].shape
    return pl.pallas_call(
        functools.partial(assemble_kernel, count, slices, by_column, rolled),
        grid_spec=pltpu.PrefetchScalarGridSpec(
            num_scalar_prefetch=1,
            grid=(1,),
            in_specs=[pl.BlockSpec((rows, width), lambda i, at: (0, 0))] * count,
            out_specs=[pl.BlockSpec(shape, lambda i, at: (0, 0)) for shape in shapes],
        ),
        out_shape=[jax.ShapeDtypeStruct(shape, F32) for shape in shapes],
        compiler_params=pltpu.CompilerParams(vmem_limit_bytes=56 * 1024 * 1024),
        cost_estimate=pl.CostEstimate(
            flops=0, bytes_accessed=6 * count * rows * width, transcendentals=0
        ),
        name="assemble_rows",
    )(offsets, *pieces)


def together(*values):
    return lax.optimization_barrier(values)


def spread_near(column):
    side = column.shape[0] // 2
    near = []
    for part in range(2):
        own = column[part * side : (part + 1) * side]
        one, two = ("x", "y") if part == 0 else ("y", "x")
        near += [own, swap(own, one), swap(own, two)]
    return near


def spread_far(near):
    zs = lax.axis_size("z")
    y, x, c = (lax.axis_index(a) for a in PLANE)
    rows = near[0].shape[0] // (zs // 2)
    pieces, offsets = [], []
    for part in range(2):
        one, two = ("x", "y") if part == 0 else ("y", "x")
        own, by_one, by_two = near[3 * part : 3 * part + 3]
        for item, at_one, at_two in (
            (own, 0, 0),
            (by_one, 1, 0),
            (by_two, 0, 1),
            (swap(by_one, two), 1, 1),
        ):
            dx, dy = (at_one, at_two) if one == "x" else (at_two, at_one)
            for dc in range(2):
                pieces.append(swap(item, "c") if dc else item)
                source = ((y ^ dy) * 2 + (x ^ dx)) * 2 + (c ^ dc)
                for z in range(zs // 2):
                    offsets.append(((part * (zs // 2) + z) * 8 + source) * rows)
    return place_rows(pieces, zs // 2, jnp.stack(offsets).astype(jnp.int32))


def shards(
    hidden_in,
    out_grad,
    segment_ids,
    row_position,
    gain_first,
    shift_first,
    qkv_weight,
    qv_bias,
    out_weight,
    out_bias,
    gain_second,
    shift_second,
    fc_weight,
    fc_bias,
    proj_weight,
    proj_bias,
):
    zs, ys, xs, cs = (lax.axis_size(a) for a in ALL)
    reps = xs * cs
    plane = ys * reps
    seqs = zs * ys
    z_at, y_at, x_at, c_at = (lax.axis_index(a) for a in ALL)
    q_at = x_at * cs + c_at
    f_at = y_at * reps + q_at
    seq_at = z_at * ys + y_at
    rows = hidden_in.shape[1]
    width = hidden_in.shape[2]
    window = rows * seqs
    capacity = 2 * rows // seqs
    halo = max(1, seqs // 4)
    ctx = (halo + 1) * rows
    padding_id = max(8, window // 256) - 1
    qkv_cols = qkv_weight.shape[1]
    ff = fc_weight.shape[1]
    ff_unit = ff // seqs // reps
    ff_own = zs * ff_unit
    shard = width // seqs

    def fc_columns(y):
        picked = []
        for z in range(zs):
            start = ((z * ys + y) * reps + q_at) * ff_unit
            picked.append(lax.dynamic_slice_in_dim(fc_weight, start, ff_unit, 1))
        return jnp.concatenate(picked, axis=1)

    if ys == 2:
        fc_mine, fc_other = fc_columns(y_at), swap(fc_columns(1 - y_at), "y")
        fc_pair = jnp.concatenate(
            [jnp.where(y_at == 0, fc_mine, fc_other), jnp.where(y_at == 0, fc_other, fc_mine)]
        )
    else:
        fc_pair = lax.all_to_all(
            jnp.stack([fc_columns(y) for y in range(ys)]), "y", 0, 0, tiled=True
        ).reshape(ys * shard, ff_own)

    places = row_position[0]
    segments = segment_ids[0]
    targets = (places // rows).reshape(seqs, rows)
    earlier = (
        lax.broadcasted_iota(jnp.int32, (rows, rows), 1)
        < lax.broadcasted_iota(jnp.int32, (rows, rows), 0)
    )
    same = (targets[:, :, None] == targets[:, None, :]) & earlier[None]
    ranks = jnp.sum(same.astype(jnp.int32), axis=2).reshape(window)
    first_row = seq_at * rows
    slots = seqs * capacity
    send_slots = lax.dynamic_slice_in_dim(places // rows * capacity + ranks, first_row, rows)
    arrive_slots = jnp.arange(window, dtype=jnp.int32) // rows * capacity + ranks
    own_places = first_row + jnp.arange(rows, dtype=jnp.int32)
    recv_slots = jnp.sum(
        jnp.where(places[None, :] == own_places[:, None], arrive_slots[None, :], 0), axis=1
    )
    slot_ids = jnp.arange(slots, dtype=jnp.int32)
    pick_send = (send_slots[:, None] == slot_ids[None, :]).astype(BF16)
    pick_recv = (recv_slots[:, None] == slot_ids[None, :]).astype(BF16)

    def exchange_first(values):
        wide = capacity + extra
        wide_ids = jnp.arange(seqs * wide, dtype=jnp.int32)
        send_wide = send_slots // capacity * wide + send_slots % capacity
        recv_wide = recv_slots // capacity * wide + recv_slots % capacity
        pick_rows = (send_wide[:, None] == wide_ids[None, :]).astype(BF16)
        pick_small = (wide_ids % wide - capacity)[None, :] == jnp.arange(extra)[:, None]
        packed = dot(
            jnp.concatenate([pick_rows, pick_small.astype(BF16)], axis=0),
            jnp.concatenate([values, small_rows], axis=0),
            TN,
        )
        packed = packed.astype(BF16).reshape(seqs, wide, width)
        moved = lax.all_to_all(packed, SEQ, split_axis=0, concat_axis=0, tiled=True)
        return moved, recv_wide, wide_ids

    def arrive_first(moved, recv_wide, wide_ids):
        pick_wide = (recv_wide[:, None] == wide_ids[None, :]).astype(BF16)
        every = moved[:, capacity:].reshape(seqs, extra * width)[:, : small.shape[0]]
        return dot(pick_wide, moved.reshape(wide_ids.shape[0], width), NN), every.astype(F32)

    def exchange(values, pick_out, pick_in):
        packed = dot(pick_out, values, TN).astype(BF16).reshape(seqs, capacity, values.shape[1])
        moved = lax.all_to_all(packed, SEQ, split_axis=0, concat_axis=0, tiled=True)
        return dot(pick_in, moved.reshape(slots, values.shape[1]), NN)

    def to_places(values):
        return exchange(values, pick_send, pick_recv)

    def to_stored(values):
        return exchange(values, pick_recv, pick_send)

    vectors = (
        gain_first,
        shift_first,
        qv_bias,
        out_bias,
        gain_second,
        shift_second,
        fc_bias,
        proj_bias,
    )
    small = jnp.concatenate(vectors)
    extra = -(-small.shape[0] // (8 * width)) * 8
    small_rows = jnp.pad(small, (0, extra * width - small.shape[0])).reshape(extra, width)

    def quarter(weight):
        size = weight.shape[0] // reps
        return lax.dynamic_slice_in_dim(weight, q_at * size, size, 0)

    proj_rows = quarter(proj_weight)
    parts = [slice(p * ff_own, (p + 1) * ff_own) for p in range(width // ff_own)]
    fc_rows = ys * shard
    units_part = jnp.concatenate([fc_pair] + [proj_rows[:, part] for part in parts], axis=0)
    with jax.named_scope("attention_weights"):
        if small_plane():
            stored, quarters = together(
                hidden_in[0],
                jnp.concatenate([quarter(qkv_weight), quarter(out_weight)], axis=1),
            )
            columns = lax.all_gather(quarters, "z", axis=0, tiled=True)
        else:
            stored = hidden_in[0]
            columns = lax.all_gather(quarter(qkv_weight), ALL, axis=0, tiled=True)
    with jax.named_scope("hidden_to_places"):
        moved, *picks = exchange_first(stored)
    units_part, grad_stored, columns, moved = together(
        units_part, out_grad[0], columns, moved
    )
    with jax.named_scope("units_gather"):
        hidden_units = lax.all_gather(units_part, "z", axis=0, tiled=False)

    with jax.named_scope("hidden_to_places"):
        inputs, small_all = arrive_first(moved, *picks)
    if small_plane():
        qkv_near = spread_near(columns[:, :qkv_cols])
        out_column, *qkv_near = together(columns[:, qkv_cols:], *qkv_near)
        with jax.named_scope("qkv_gather"):
            full_qkv = spread_far(qkv_near)
        with jax.named_scope("out_gather"):
            full_out = spread_far(spread_near(out_column))
    else:
        full_qkv = columns
        full_out = lax.all_gather(quarter(out_weight), ALL, axis=0, tiled=True)
    wholes = []
    at = 0
    for item in vectors:
        wholes.append(small_all[:, at : at + item.shape[0]].reshape(-1))
        at += item.shape[0]
    gain1, shift1, qv_full, out_shift, gain2, shift2, fc_shift, proj_shift = wholes
    fc_shift_own = lax.dynamic_slice(
        fc_shift.reshape(zs, ys, reps, ff_unit), (0, y_at, q_at, 0), (zs, 1, 1, ff_unit)
    ).reshape(ff_own)

    unit1, rstd1 = norm_parts(inputs)
    normed1 = (unit1 * gain1 + shift1).astype(BF16)
    projected = dot(normed1, full_qkv, NN)
    queries = (projected[:, :width] + qv_full[:width]).astype(BF16)
    kv_shift = jnp.concatenate([jnp.zeros((HD,), F32), qv_full[width:]])
    kv_own = (projected[:, width:] + kv_shift).astype(BF16)
    blocks = []
    for back in range(halo, 0, -1):
        pairs = [(i, i + back) for i in range(seqs - back)]
        blocks.append(lax.ppermute(kv_own, SEQ, pairs))
    kv_ctx = jnp.concatenate(blocks + [kv_own], axis=0)
    with jax.named_scope("grad_to_places"):
        grad_f32 = to_places(grad_stored)
    queries, grad_f32 = together(queries, grad_f32)
    seg_own = lax.dynamic_slice_in_dim(segments, first_row, rows)[:, None]
    seg_padded = jnp.concatenate([jnp.full((halo * rows,), -1, jnp.int32), segments])
    seg_ctx = lax.dynamic_slice_in_dim(seg_padded, first_row, ctx)[None, :]
    attended_low, attended, norms = attention_forward(
        queries, kv_ctx, seg_own, seg_ctx, padding_id
    )
    grad_low = grad_f32.astype(BF16)
    with jax.named_scope("grad_gather"):
        grad_all = gather_plane(grad_low)
    attended_low, grad_all = together(attended_low, grad_all)
    middle = inputs + (dot(attended_low, full_out, NN) + out_shift)

    unit2, rstd2 = norm_parts(middle)
    normed2 = (unit2 * gain2 + shift2).astype(BF16)
    with jax.named_scope("normed2_gather"):
        normed2_all = gather_plane(normed2)
    with jax.named_scope("both_gather"):
        both_low, normed2_all = together(
            jnp.concatenate([normed1, attended_low], axis=1), normed2_all
        )
        both_all = lax.all_gather(both_low, PLANE, axis=0, tiled=True)
    fc_own = hidden_units[:, :fc_rows].reshape(width, ff_own)
    proj_parts = [
        hidden_units[:, fc_rows + p * ff_unit : fc_rows + (p + 1) * ff_unit].reshape(ff_own, ff_own)
        for p in range(len(parts))
    ]

    pre_act = dot(normed2_all, fc_own, NN) + fc_shift_own
    act, slope = gelu_pair(pre_act)
    act_low = act.astype(BF16)
    grad_act = sum(dot(grad_all[:, part], own, NT) for part, own in zip(parts, proj_parts))
    grad_pre = (grad_act * slope).astype(BF16)
    dfc_bias_own = jnp.sum(grad_pre.astype(F32), axis=0)

    def over_z(partial):
        return lax.psum_scatter(partial, "z", scatter_dimension=0, tiled=True)

    unit_terms = [dot(normed2_all, grad_pre, TN).reshape(zs, fc_rows, ff_own)]
    for part in parts:
        unit_terms.append(dot(act_low, grad_all[:, part], TN).reshape(zs, ff_unit, ff_own))
    unit_terms = jnp.concatenate(unit_terms, axis=1).astype(BF16).reshape(-1, ff_own)
    unit_terms, both_all, act_late = together(unit_terms, both_all, act_low)
    normed1_all, attended_all = both_all[:, :width], both_all[:, width:]
    with jax.named_scope("grad_normed2_scatter"):
        grad_normed2, scattered = scatter_plane(
            lambda first, count: dot(grad_pre[first : first + count], fc_own, NT),
            rows,
            unit_terms,
        )
    units = over_z(unit_terms)
    with jax.named_scope("mlp_out_scatter"):
        mlp_out, _ = scatter_plane(
            lambda first, count: jnp.concatenate(
                [dot(act_late[first : first + count], own, NN) for own in proj_parts], axis=1
            ),
            rows,
            scattered,
        )
    dgain2 = jnp.sum(grad_normed2 * unit2, axis=0)
    dshift2 = jnp.sum(grad_normed2, axis=0)
    dproj_bias = jnp.sum(grad_f32, axis=0)
    grad_middle = grad_f32 + norm_back(grad_normed2, unit2, rstd2, gain2)

    grad_branch = grad_middle.astype(BF16)
    dout_bias = jnp.sum(grad_branch.astype(F32), axis=0)
    grad_attended = dot(grad_branch, full_out, NT).astype(BF16)
    dq, dkv_ctx = attention_backward(
        queries, grad_attended, attended, norms, kv_ctx, seg_own, seg_ctx, padding_id
    )
    result = (middle + mlp_out + proj_shift).astype(BF16)
    with jax.named_scope("result_to_stored"):
        hidden_out = to_stored(result).astype(BF16)
    dkv = dkv_ctx[halo * rows :]
    for back in range(1, halo + 1):
        pairs = [(i + back, i) for i in range(seqs - back)]
        term = dkv_ctx[(halo - back) * rows : (halo - back + 1) * rows].astype(BF16)
        dkv = dkv + lax.ppermute(term, SEQ, pairs).astype(F32)
    grad_qkv = jnp.concatenate([dq, dkv.astype(BF16)], axis=1)
    grad_normed1 = dot(grad_qkv, full_qkv, NT)
    dgain1 = jnp.sum(grad_normed1 * unit1, axis=0)
    dshift1 = jnp.sum(grad_normed1, axis=0)
    grad_in = grad_middle + norm_back(grad_normed1, unit1, rstd1, gain1)
    with jax.named_scope("input_grad_to_stored"):
        input_grad = to_stored(grad_in.astype(BF16))
    grad_qkv_f32 = grad_qkv.astype(F32)
    dqv_bias = jnp.concatenate(
        [jnp.sum(grad_qkv_f32[:, :width], axis=0), jnp.sum(grad_qkv_f32[:, width + HD :], axis=0)]
    )

    def columns_of_plane(values):
        parts = [values[:, :width].reshape(rows, plane, width // plane)]
        if values.shape[1] > width:
            parts.append(values[:, width:].reshape(rows, plane, -1))
        sent = jnp.concatenate(parts, axis=2).transpose(1, 0, 2)
        cols = sent.shape[2]
        return lax.all_to_all(sent, PLANE, split_axis=0, concat_axis=0, tiled=True).reshape(
            plane * rows, cols
        )

    dout_own = dot(attended_all, columns_of_plane(grad_branch), TN).astype(BF16)
    dqkv_own = dot(normed1_all, columns_of_plane(grad_qkv), TN).astype(BF16)

    first_row_y = y_at * shard
    flipped = (1 - y_at) * shard

    def rows_of_y(partial):
        cols = partial.shape[1]
        if ys == 2:
            kept = lax.dynamic_slice_in_dim(partial, first_row_y, shard, 0)
            return [kept, swap(lax.dynamic_slice_in_dim(partial, flipped, shard, 0), "y")]
        moved = lax.all_to_all(
            partial.reshape(ys, shard, cols), "y", split_axis=0, concat_axis=0, tiled=True
        )
        return [moved[y] for y in range(ys)]

    def near_rep(pieces):
        return pieces + [swap(item, "x") for item in pieces]

    def far_rep(pieces):
        return pieces + [swap(item, "c") for item in pieces]

    def sources(count):
        found = []
        for dc, dx, dy in itertools.product(range(2), range(2), range(count)):
            y = (y_at ^ dy) if ys == 2 else dy
            found.append((y * reps if count > 1 else 0) + (x_at ^ dx) * cs + (c_at ^ dc))
        return jnp.stack(found).astype(jnp.int32)

    proj_near = near_rep([units[fc_rows:]])
    fc_near = near_rep(rows_of_y(units[:fc_rows]))
    head_terms, input_grad, hidden_out, proj_near, fc_near = together(
        jnp.concatenate([dqkv_own, dout_own], axis=1), input_grad, hidden_out, proj_near, fc_near
    )
    with jax.named_scope("proj_grad_rows"):
        proj_pieces = far_rep(proj_near)
        dproj_weight = assemble(
            proj_pieces,
            [(p * ff_unit, ff_unit, 0, ff_own, 0, p * ff_own) for p in range(len(parts))],
            [(ff // seqs, width)],
            sources(1) * ff_unit,
        )[0]
    with jax.named_scope("fc_grad_rows"):
        fc_pieces = far_rep(fc_near)
        if small_plane():
            dfc_weight = assemble(
                fc_pieces,
                [(0, shard, z * ff_unit, ff_unit, 0, z * plane * ff_unit) for z in range(zs)],
                [(shard, ff)],
                sources(ys) * ff_unit,
                by_column=True,
            )[0]
        else:
            stacked = jnp.stack(fc_pieces).reshape(plane, shard, zs, ff_unit)
            order = jnp.argsort(sources(ys))
            dfc_weight = (
                stacked[order].transpose(1, 2, 0, 3).reshape(shard, ff).astype(F32)
            )
    dfc_bias = lax.dynamic_update_slice(
        jnp.zeros((zs, ys, reps, ff_unit), F32),
        dfc_bias_own.reshape(zs, 1, 1, ff_unit),
        (0, y_at, q_at, 0),
    ).reshape(ff)
    mids = (dout_bias, dgain2, dshift2, dfc_bias, dproj_bias)
    lasts = (dgain1, dshift1, dqv_bias)

    def reduce_small(items):
        total = jnp.concatenate(items).reshape(-1, HD)
        if small_plane():
            for axis in ("c", "x", "y"):
                total = total + swap(total, axis)
            total = sum([shift(total, "z", away) for away in range(1, zs)], total)
        else:
            total = lax.psum(total, ALL)
        total = total.reshape(-1)
        outs, at = [], 0
        for item in items:
            size = item.shape[0] // seqs
            outs.append(lax.dynamic_slice_in_dim(total, at + seq_at * size, size))
            at += item.shape[0]
        return outs

    mids = reduce_small(mids)
    lasts = reduce_small(lasts)
    with jax.named_scope("attention_grad_rows"):
        heads, dfc_weight, dproj_weight, mids, lasts = together(
            over_z(head_terms), dfc_weight, dproj_weight, mids, lasts
        )
        dout_bias, dgain2, dshift2, dfc_bias, dproj_bias = mids
        dgain1, dshift1, dqv_bias = lasts
        head_pieces = far_rep(near_rep(rows_of_y(heads)))
        q_cols, kv_cols = width // plane, 2 * HD // plane
        if small_plane():
            dqkv_weight, dout_weight = assemble(
                head_pieces,
                [(0, shard, 0, q_cols, 0, 0), (0, shard, q_cols + kv_cols, q_cols, 1, 0)],
                [(shard, qkv_cols), (shard, width)],
                sources(ys) * q_cols,
                by_column=True,
                rolled=(q_cols, kv_cols, 0, width),
            )
        else:
            stacked = jnp.stack(head_pieces)[jnp.argsort(sources(ys))].transpose(1, 0, 2)
            stacked = stacked.astype(F32)
            dq_cols = stacked[:, :, :q_cols].reshape(shard, width)
            dkv_cols = stacked[:, :, q_cols : q_cols + kv_cols].reshape(shard, 2 * HD)
            dqkv_weight = jnp.concatenate([dq_cols, dkv_cols], axis=1)
            dout_weight = stacked[:, :, q_cols + kv_cols :].reshape(shard, width)

    return (
        hidden_out[None],
        input_grad[None],
        dgain1,
        dshift1,
        dqkv_weight,
        dqv_bias,
        dout_weight,
        dout_bias,
        dgain2,
        dshift2,
        dfc_weight,
        dfc_bias,
        dproj_weight,
        dproj_bias,
    )


def solution(mesh):
    seqs, reps = mesh.shape["seq"], mesh.shape["rep"]
    grid = Mesh(mesh.devices.reshape(4, seqs // 4, reps // 2, 2), ALL)
    wide = P(REP, SEQ, None)
    table = P(REP, None)
    vector = P(SEQ)
    matrix = P(SEQ, None)
    return jax.shard_map(
        shards,
        mesh=grid,
        in_specs=(
            wide,
            wide,
            table,
            table,
            vector,
            vector,
            matrix,
            vector,
            matrix,
            vector,
            vector,
            vector,
            matrix,
            vector,
            matrix,
            vector,
        ),
        out_specs=(
            wide,
            wide,
            vector,
            vector,
            matrix,
            vector,
            matrix,
            vector,
            vector,
            vector,
            matrix,
            vector,
            matrix,
            vector,
        ),
        check_vma=False,
    )
```

```python
import functools
import itertools
import math

import jax
import jax.numpy as jnp
from jax import lax
from jax.experimental import pallas as pl
from jax.experimental.pallas import tpu as pltpu
from jax.sharding import Mesh
from jax.sharding import PartitionSpec as P

HD = 128
EPSILON = 1e-05
NEGATIVE = -1e30
SCALE = 1.0 / math.sqrt(HD)
LOG2E = math.log2(math.e)
GELU_C = math.sqrt(2.0 / math.pi)
SEQ = ("z", "y")
REP = ("x", "c")
PLANE = ("y", "x", "c")
ALL = ("z", "y", "x", "c")
BF16 = jnp.bfloat16
F32 = jnp.float32
HEADS_STEP = 2


def dot(left, right, dims):
    return lax.dot_general(left, right, (dims, ((), ())), preferred_element_type=F32)


NN = ((1,), (0,))
NT = ((1,), (1,))
TN = ((0,), (0,))


def attention_bias(seg_own, seg_ctx, padding_id, rows, ctx):
    t = lax.broadcasted_iota(jnp.int32, (rows, ctx), 0)
    u = lax.broadcasted_iota(jnp.int32, (rows, ctx), 1)
    allowed = (seg_own == seg_ctx) & (u <= t + (ctx - rows)) & (seg_own != padding_id)
    return jnp.where(allowed, 0.0, NEGATIVE).astype(F32)


def forward_kernel(padding_id, q_ref, kv_ref, own_ref, ctx_ref, low_ref, att_ref, norm_ref, bias):
    rows, ctx = bias.shape

    @pl.when(pl.program_id(0) == 0)
    def _():
        bias[...] = attention_bias(own_ref[...], ctx_ref[...], padding_id, rows, ctx)

    live = own_ref[...] != padding_id
    keys = kv_ref[:, :HD]
    values = kv_ref[:, HD:]
    for head in range(HEADS_STEP):
        lanes = slice(head * HD, (head + 1) * HD)
        scores = dot(q_ref[:, lanes], keys, NT) * (SCALE * LOG2E) + bias[...]
        top = jnp.max(scores, axis=1, keepdims=True)
        weights = jnp.exp2(scores - top)
        sums = jnp.sum(weights, axis=1, keepdims=True)
        mixed = dot(weights.astype(BF16), values, NN)
        attended = jnp.where(live, mixed / sums, 0.0)
        att_ref[:, lanes] = attended
        low_ref[:, lanes] = attended.astype(BF16)
        norm = jnp.where(live, top + jnp.log2(sums), 0.0)
        norm_ref[:, lanes] = jnp.broadcast_to(norm, (rows, HD))


def attention_forward(queries, kv_ctx, seg_own, seg_ctx, padding_id):
    rows, width = queries.shape
    ctx = kv_ctx.shape[0]
    step = HEADS_STEP * HD
    tile = pl.BlockSpec((rows, step), lambda h: (0, h))
    return pl.pallas_call(
        functools.partial(forward_kernel, padding_id),
        grid=(width // step,),
        in_specs=[
            tile,
            pl.BlockSpec((ctx, 2 * HD), lambda h: (0, 0)),
            pl.BlockSpec((rows, 1), lambda h: (0, 0)),
            pl.BlockSpec((1, ctx), lambda h: (0, 0)),
        ],
        out_specs=[tile, tile, tile],
        out_shape=[
            jax.ShapeDtypeStruct((rows, width), BF16),
            jax.ShapeDtypeStruct((rows, width), F32),
            jax.ShapeDtypeStruct((rows, width), F32),
        ],
        scratch_shapes=[pltpu.VMEM((rows, ctx), F32)],
        compiler_params=pltpu.CompilerParams(vmem_limit_bytes=40 * 1024 * 1024),
        cost_estimate=pl.CostEstimate(
            flops=4 * rows * ctx * width,
            bytes_accessed=12 * rows * width,
            transcendentals=rows * ctx * width // HD,
        ),
        name="attention_forward",
    )(queries, kv_ctx, seg_own, seg_ctx)


def backward_kernel(
    padding_id, q_ref, g_ref, att_ref, norm_ref, kv_ref, own_ref, ctx_ref, dq_ref, dkv_ref, bias
):
    rows, ctx = bias.shape

    @pl.when(pl.program_id(0) == 0)
    def _():
        bias[...] = attention_bias(own_ref[...], ctx_ref[...], padding_id, rows, ctx)
        dkv_ref[...] = jnp.zeros_like(dkv_ref)

    keys = kv_ref[:, :HD]
    values = kv_ref[:, HD:]
    for head in range(HEADS_STEP):
        lanes = slice(head * HD, (head + 1) * HD)
        q = q_ref[:, lanes]
        g = g_ref[:, lanes]
        delta = jnp.sum(g.astype(F32) * att_ref[:, lanes], axis=1, keepdims=True)
        norm = norm_ref[:, head * HD : head * HD + 1]
        scores = dot(q, keys, NT) * (SCALE * LOG2E) + bias[...]
        prob = jnp.exp2(scores - norm)
        grad_prob = dot(g, values, NT)
        grad_scores = (prob * (grad_prob - delta) * SCALE).astype(BF16)
        dq_ref[:, lanes] = dot(grad_scores, keys, NN).astype(BF16)
        dkv_ref[:, :HD] += dot(grad_scores, q, TN)
        dkv_ref[:, HD:] += dot(prob.astype(BF16), g, TN)


def attention_backward(queries, grads, attended, norms, kv_ctx, seg_own, seg_ctx, padding_id):
    rows, width = queries.shape
    ctx = kv_ctx.shape[0]
    step = HEADS_STEP * HD
    tile = pl.BlockSpec((rows, step), lambda h: (0, h))
    whole = pl.BlockSpec((ctx, 2 * HD), lambda h: (0, 0))
    return pl.pallas_call(
        functools.partial(backward_kernel, padding_id),
        grid=(width // step,),
        in_specs=[
            tile,
            tile,
            tile,
            tile,
            whole,
            pl.BlockSpec((rows, 1), lambda h: (0, 0)),
            pl.BlockSpec((1, ctx), lambda h: (0, 0)),
        ],
        out_specs=[tile, whole],
        out_shape=[
            jax.ShapeDtypeStruct((rows, width), BF16),
            jax.ShapeDtypeStruct((ctx, 2 * HD), F32),
        ],
        scratch_shapes=[pltpu.VMEM((rows, ctx), F32)],
        compiler_params=pltpu.CompilerParams(vmem_limit_bytes=48 * 1024 * 1024),
        cost_estimate=pl.CostEstimate(
            flops=10 * rows * ctx * width,
            bytes_accessed=14 * rows * width,
            transcendentals=rows * ctx * width // HD,
        ),
        name="attention_backward",
    )(queries, grads, attended, norms, kv_ctx, seg_own, seg_ctx)


def norm_parts(values):
    center = values - jnp.mean(values, axis=-1, keepdims=True)
    spread = jnp.mean(center * center, axis=-1, keepdims=True)
    rstd = lax.rsqrt(spread + EPSILON)
    return center * rstd, rstd


def norm_back(grad, unit, rstd, gain):
    scaled = grad * gain
    mean_g = jnp.mean(scaled, axis=-1, keepdims=True)
    mean_gu = jnp.mean(scaled * unit, axis=-1, keepdims=True)
    return rstd * (scaled - mean_g - unit * mean_gu)


def gelu_pair(v):
    inner = jnp.tanh(GELU_C * (v + 0.044715 * v * v * v))
    value = 0.5 * v * (1.0 + inner)
    slope = 0.5 * (1.0 + inner) + 0.5 * v * (1.0 - inner * inner) * GELU_C * (
        1.0 + 3.0 * 0.044715 * v * v
    )
    return value, slope


def swap(block, axis):
    return lax.ppermute(block, axis, [(0, 1), (1, 0)])


def pair(block, axis):
    if lax.axis_size(axis) != 2:
        return lax.all_gather(block, axis, axis=0, tiled=False)
    other = swap(block, axis)
    first = lax.axis_index(axis) == 0
    return jnp.stack([jnp.where(first, block, other), jnp.where(first, other, block)])


def small_plane():
    return lax.axis_size("y") == 2


def plane_pieces(block):
    if not small_plane():
        return [lax.all_gather(block, PLANE, axis=0, tiled=True)]
    half = block.shape[0] // 2
    top, low = block[:half], block[half:]
    top_x, low_y = swap(top, "x"), swap(low, "y")
    top_y, low_x = swap(top, "y"), swap(low, "x")
    top_xy, low_yx = swap(top_x, "y"), swap(low_y, "x")
    near = [top, top_y, top_x, top_xy, low, low_x, low_y, low_yx]
    return near + [swap(item, "c") for item in near]


def join_kernel(count, *refs):
    rows = refs[0].shape[0]
    for i in range(count):
        refs[count][i * rows : (i + 1) * rows, :] = refs[i][...]


def join_rows(pieces):
    count = len(pieces)
    if count == 1:
        return pieces[0]
    rows, width = pieces[0].shape
    return pl.pallas_call(
        functools.partial(join_kernel, count),
        grid=(1,),
        in_specs=[pl.BlockSpec((rows, width), lambda i: (0, 0))] * count,
        out_specs=pl.BlockSpec((count * rows, width), lambda i: (0, 0)),
        out_shape=jax.ShapeDtypeStruct((count * rows, width), pieces[0].dtype),
        compiler_params=pltpu.CompilerParams(vmem_limit_bytes=56 * 1024 * 1024),
        cost_estimate=pl.CostEstimate(
            flops=0, bytes_accessed=4 * count * rows * width, transcendentals=0
        ),
        name="join_rows",
    )(*pieces)


def gather_plane(block):
    return join_rows(plane_pieces(block))


def scatter_plane(partial, rows, hold=None):
    total = rows * lax.axis_size("y") * lax.axis_size("x") * lax.axis_size("c")
    if not small_plane():
        return lax.psum_scatter(
            partial(0, total).astype(BF16), PLANE, scatter_dimension=0, tiled=True
        ).astype(F32), hold
    side = total // 2
    got = swap(partial(side, side).astype(BF16), "c")
    both = (partial(0, side) + got.astype(F32)).astype(BF16)
    if hold is not None:
        both, _ = together(both, hold)
    top, low = both[: side // 2], both[side // 2 :]
    got_top, got_low = swap(top[rows:], "x"), swap(low[rows:], "y")
    top = (top[:rows].astype(F32) + got_top.astype(F32)).astype(BF16)
    low = (low[:rows].astype(F32) + got_low.astype(F32)).astype(BF16)
    half = rows // 2
    got_top, got_low = swap(top[half:], "y"), swap(low[half:], "x")
    sums = jnp.concatenate(
        [
            top[:half].astype(F32) + got_top.astype(F32),
            low[:half].astype(F32) + got_low.astype(F32),
        ],
        axis=0,
    )
    return sums, got_low


def shift(block, axis, by):
    count = math.prod(lax.axis_size(a) for a in ([axis] if isinstance(axis, str) else axis))
    return lax.ppermute(block, axis, [(i, (i + by) % count) for i in range(count)])


def place_kernel(count, parts, offsets, *refs):
    out = refs[count]
    for i in range(count):
        rows = refs[i].shape[0] // parts
        for j in range(parts):
            start = pl.multiple_of(offsets[i * parts + j], rows)
            out[pl.ds(start, rows), :] = refs[i][j * rows : (j + 1) * rows, :]


def place_rows(pieces, parts, offsets):
    count = len(pieces)
    rows, width = pieces[0].shape
    return pl.pallas_call(
        functools.partial(place_kernel, count, parts),
        grid_spec=pltpu.PrefetchScalarGridSpec(
            num_scalar_prefetch=1,
            grid=(1,),
            in_specs=[pl.BlockSpec((rows, width), lambda i, at: (0, 0))] * count,
            out_specs=pl.BlockSpec((count * rows, width), lambda i, at: (0, 0)),
        ),
        out_shape=jax.ShapeDtypeStruct((count * rows, width), pieces[0].dtype),
        compiler_params=pltpu.CompilerParams(vmem_limit_bytes=56 * 1024 * 1024),
        cost_estimate=pl.CostEstimate(
            flops=0, bytes_accessed=4 * count * rows * width, transcendentals=0
        ),
        name="place_rows",
    )(offsets, *pieces)


def assemble_kernel(count, slices, by_column, rolled, offsets, *refs):
    outs = refs[count:]
    if rolled is not None:
        total = jnp.zeros((refs[0].shape[0], 2 * HD), F32)
    for i in range(count):
        for row, rows, first, cols, target, base in slices:
            values = refs[i][row : row + rows, first : first + cols].astype(F32)
            if by_column:
                start = pl.multiple_of(offsets[i] + base, HD)
                outs[target][:, pl.ds(start, cols)] = values
            else:
                start = pl.multiple_of(offsets[i], rows)
                outs[target][pl.ds(start, rows), base : base + cols] = values
        if rolled is not None:
            first, wide, target, at = rolled
            narrow = refs[i][:, first : first + wide].astype(F32)
            padded = jnp.concatenate(
                [narrow, jnp.zeros((narrow.shape[0], 2 * HD - wide), F32)], axis=1
            )
            total = total + pltpu.roll(padded, offsets[i] * wide // slices[0][3], 1)
    if rolled is not None:
        outs[target][:, at : at + 2 * HD] = total


def assemble(pieces, slices, shapes, offsets, by_column=False, rolled=None):
    count = len(pieces)
    rows, width = pieces[0].shape
    return pl.pallas_call(
        functools.partial(assemble_kernel, count, slices, by_column, rolled),
        grid_spec=pltpu.PrefetchScalarGridSpec(
            num_scalar_prefetch=1,
            grid=(1,),
            in_specs=[pl.BlockSpec((rows, width), lambda i, at: (0, 0))] * count,
            out_specs=[pl.BlockSpec(shape, lambda i, at: (0, 0)) for shape in shapes],
        ),
        out_shape=[jax.ShapeDtypeStruct(shape, F32) for shape in shapes],
        compiler_params=pltpu.CompilerParams(vmem_limit_bytes=56 * 1024 * 1024),
        cost_estimate=pl.CostEstimate(
            flops=0, bytes_accessed=6 * count * rows * width, transcendentals=0
        ),
        name="assemble_rows",
    )(offsets, *pieces)


def together(*values):
    return lax.optimization_barrier(values)


def spread_near(column):
    side = column.shape[0] // 2
    near = []
    for part in range(2):
        own = column[part * side : (part + 1) * side]
        one, two = ("x", "y") if part == 0 else ("y", "x")
        near += [own, swap(own, one), swap(own, two)]
    return near


def spread_far(near):
    zs = lax.axis_size("z")
    y, x, c = (lax.axis_index(a) for a in PLANE)
    rows = near[0].shape[0] // (zs // 2)
    pieces, offsets = [], []
    for part in range(2):
        one, two = ("x", "y") if part == 0 else ("y", "x")
        own, by_one, by_two = near[3 * part : 3 * part + 3]
        for item, at_one, at_two in (
            (own, 0, 0),
            (by_one, 1, 0),
            (by_two, 0, 1),
            (swap(by_one, two), 1, 1),
        ):
            dx, dy = (at_one, at_two) if one == "x" else (at_two, at_one)
            for dc in range(2):
                pieces.append(swap(item, "c") if dc else item)
                source = ((y ^ dy) * 2 + (x ^ dx)) * 2 + (c ^ dc)
                for z in range(zs // 2):
                    offsets.append(((part * (zs // 2) + z) * 8 + source) * rows)
    return place_rows(pieces, zs // 2, jnp.stack(offsets).astype(jnp.int32))


def shards(
    hidden_in,
    out_grad,
    segment_ids,
    row_position,
    gain_first,
    shift_first,
    qkv_weight,
    qv_bias,
    out_weight,
    out_bias,
    gain_second,
    shift_second,
    fc_weight,
    fc_bias,
    proj_weight,
    proj_bias,
):
    zs, ys, xs, cs = (lax.axis_size(a) for a in ALL)
    reps = xs * cs
    plane = ys * reps
    seqs = zs * ys
    z_at, y_at, x_at, c_at = (lax.axis_index(a) for a in ALL)
    q_at = x_at * cs + c_at
    f_at = y_at * reps + q_at
    seq_at = z_at * ys + y_at
    rows = hidden_in.shape[1]
    width = hidden_in.shape[2]
    window = rows * seqs
    capacity = 2 * rows // seqs
    halo = max(1, seqs // 4)
    ctx = (halo + 1) * rows
    padding_id = max(8, window // 256) - 1
    qkv_cols = qkv_weight.shape[1]
    ff = fc_weight.shape[1]
    ff_unit = ff // seqs // reps
    ff_own = zs * ff_unit
    shard = width // seqs

    def fc_columns(y):
        picked = []
        for z in range(zs):
            start = ((z * ys + y) * reps + q_at) * ff_unit
            picked.append(lax.dynamic_slice_in_dim(fc_weight, start, ff_unit, 1))
        return jnp.concatenate(picked, axis=1)

    if ys == 2:
        fc_mine, fc_other = fc_columns(y_at), swap(fc_columns(1 - y_at), "y")
        fc_pair = jnp.concatenate(
            [jnp.where(y_at == 0, fc_mine, fc_other), jnp.where(y_at == 0, fc_other, fc_mine)]
        )
    else:
        fc_pair = lax.all_to_all(
            jnp.stack([fc_columns(y) for y in range(ys)]), "y", 0, 0, tiled=True
        ).reshape(ys * shard, ff_own)

    places = row_position[0]
    segments = segment_ids[0]
    targets = (places // rows).reshape(seqs, rows)
    earlier = (
        lax.broadcasted_iota(jnp.int32, (rows, rows), 1)
        < lax.broadcasted_iota(jnp.int32, (rows, rows), 0)
    )
    same = (targets[:, :, None] == targets[:, None, :]) & earlier[None]
    ranks = jnp.sum(same.astype(jnp.int32), axis=2).reshape(window)
    first_row = seq_at * rows
    slots = seqs * capacity
    send_slots = lax.dynamic_slice_in_dim(places // rows * capacity + ranks, first_row, rows)
    arrive_slots = jnp.arange(window, dtype=jnp.int32) // rows * capacity + ranks
    own_places = first_row + jnp.arange(rows, dtype=jnp.int32)
    recv_slots = jnp.sum(
        jnp.where(places[None, :] == own_places[:, None], arrive_slots[None, :], 0), axis=1
    )
    slot_ids = jnp.arange(slots, dtype=jnp.int32)
    pick_send = (send_slots[:, None] == slot_ids[None, :]).astype(BF16)
    pick_recv = (recv_slots[:, None] == slot_ids[None, :]).astype(BF16)

    def exchange_first(values):
        wide = capacity + extra
        wide_ids = jnp.arange(seqs * wide, dtype=jnp.int32)
        send_wide = send_slots // capacity * wide + send_slots % capacity
        recv_wide = recv_slots // capacity * wide + recv_slots % capacity
        pick_rows = (send_wide[:, None] == wide_ids[None, :]).astype(BF16)
        pick_small = (wide_ids % wide - capacity)[None, :] == jnp.arange(extra)[:, None]
        packed = dot(
            jnp.concatenate([pick_rows, pick_small.astype(BF16)], axis=0),
            jnp.concatenate([values, small_rows], axis=0),
            TN,
        )
        packed = packed.astype(BF16).reshape(seqs, wide, width)
        moved = lax.all_to_all(packed, SEQ, split_axis=0, concat_axis=0, tiled=True)
        return moved, recv_wide, wide_ids

    def arrive_first(moved, recv_wide, wide_ids):
        pick_wide = (recv_wide[:, None] == wide_ids[None, :]).astype(BF16)
        every = moved[:, capacity:].reshape(seqs, extra * width)[:, : small.shape[0]]
        return dot(pick_wide, moved.reshape(wide_ids.shape[0], width), NN), every.astype(F32)

    def exchange(values, pick_out, pick_in):
        packed = dot(pick_out, values, TN).astype(BF16).reshape(seqs, capacity, values.shape[1])
        moved = lax.all_to_all(packed, SEQ, split_axis=0, concat_axis=0, tiled=True)
        return dot(pick_in, moved.reshape(slots, values.shape[1]), NN)

    def to_places(values):
        return exchange(values, pick_send, pick_recv)

    def to_stored(values):
        return exchange(values, pick_recv, pick_send)

    vectors = (
        gain_first,
        shift_first,
        qv_bias,
        out_bias,
        gain_second,
        shift_second,
        fc_bias,
        proj_bias,
    )
    small = jnp.concatenate(vectors)
    extra = -(-small.shape[0] // (8 * width)) * 8
    small_rows = jnp.pad(small, (0, extra * width - small.shape[0])).reshape(extra, width)

    def quarter(weight):
        size = weight.shape[0] // reps
        return lax.dynamic_slice_in_dim(weight, q_at * size, size, 0)

    proj_rows = quarter(proj_weight)
    parts = [slice(p * ff_own, (p + 1) * ff_own) for p in range(width // ff_own)]
    fc_rows = ys * shard
    units_part = jnp.concatenate([fc_pair] + [proj_rows[:, part] for part in parts], axis=0)
    with jax.named_scope("attention_weights"):
        if small_plane():
            stored, quarters = together(
                hidden_in[0],
                jnp.concatenate([quarter(qkv_weight), quarter(out_weight)], axis=1),
            )
            columns = lax.all_gather(quarters, "z", axis=0, tiled=True)
        else:
            stored = hidden_in[0]
            columns = lax.all_gather(quarter(qkv_weight), ALL, axis=0, tiled=True)
    with jax.named_scope("hidden_to_places"):
        moved, *picks = exchange_first(stored)
    units_part, grad_stored, columns, moved = together(
        units_part, out_grad[0], columns, moved
    )
    with jax.named_scope("units_gather"):
        hidden_units = lax.all_gather(units_part, "z", axis=0, tiled=False)

    with jax.named_scope("hidden_to_places"):
        inputs, small_all = arrive_first(moved, *picks)
    if small_plane():
        qkv_near = spread_near(columns[:, :qkv_cols])
        out_column, *qkv_near = together(columns[:, qkv_cols:], *qkv_near)
        with jax.named_scope("qkv_gather"):
            full_qkv = spread_far(qkv_near)
        with jax.named_scope("out_gather"):
            full_out = spread_far(spread_near(out_column))
    else:
        full_qkv = columns
        full_out = lax.all_gather(quarter(out_weight), ALL, axis=0, tiled=True)
    wholes = []
    at = 0
    for item in vectors:
        wholes.append(small_all[:, at : at + item.shape[0]].reshape(-1))
        at += item.shape[0]
    gain1, shift1, qv_full, out_shift, gain2, shift2, fc_shift, proj_shift = wholes
    fc_shift_own = lax.dynamic_slice(
        fc_shift.reshape(zs, ys, reps, ff_unit), (0, y_at, q_at, 0), (zs, 1, 1, ff_unit)
    ).reshape(ff_own)

    unit1, rstd1 = norm_parts(inputs)
    normed1 = (unit1 * gain1 + shift1).astype(BF16)
    projected = dot(normed1, full_qkv, NN)
    queries = (projected[:, :width] + qv_full[:width]).astype(BF16)
    kv_shift = jnp.concatenate([jnp.zeros((HD,), F32), qv_full[width:]])
    kv_own = (projected[:, width:] + kv_shift).astype(BF16)
    blocks = []
    for back in range(halo, 0, -1):
        pairs = [(i, i + back) for i in range(seqs - back)]
        blocks.append(lax.ppermute(kv_own, SEQ, pairs))
    kv_ctx = jnp.concatenate(blocks + [kv_own], axis=0)
    with jax.named_scope("grad_to_places"):
        grad_f32 = to_places(grad_stored)
    queries, grad_f32 = together(queries, grad_f32)
    seg_own = lax.dynamic_slice_in_dim(segments, first_row, rows)[:, None]
    seg_padded = jnp.concatenate([jnp.full((halo * rows,), -1, jnp.int32), segments])
    seg_ctx = lax.dynamic_slice_in_dim(seg_padded, first_row, ctx)[None, :]
    attended_low, attended, norms = attention_forward(
        queries, kv_ctx, seg_own, seg_ctx, padding_id
    )
    grad_low = grad_f32.astype(BF16)
    with jax.named_scope("grad_gather"):
        grad_all = gather_plane(grad_low)
    attended_low, grad_all = together(attended_low, grad_all)
    middle = inputs + (dot(attended_low, full_out, NN) + out_shift)

    unit2, rstd2 = norm_parts(middle)
    normed2 = (unit2 * gain2 + shift2).astype(BF16)
    with jax.named_scope("normed2_gather"):
        normed2_all = gather_plane(normed2)
    with jax.named_scope("both_gather"):
        both_low, normed2_all = together(
            jnp.concatenate([normed1, attended_low], axis=1), normed2_all
        )
        both_all = lax.all_gather(both_low, PLANE, axis=0, tiled=True)
    fc_own = hidden_units[:, :fc_rows].reshape(width, ff_own)
    proj_parts = [
        hidden_units[:, fc_rows + p * ff_unit : fc_rows + (p + 1) * ff_unit].reshape(ff_own, ff_own)
        for p in range(len(parts))
    ]

    pre_act = dot(normed2_all, fc_own, NN) + fc_shift_own
    act, slope = gelu_pair(pre_act)
    act_low = act.astype(BF16)
    grad_act = sum(dot(grad_all[:, part], own, NT) for part, own in zip(parts, proj_parts))
    grad_pre = (grad_act * slope).astype(BF16)
    dfc_bias_own = jnp.sum(grad_pre.astype(F32), axis=0)

    def over_z(partial):
        return lax.psum_scatter(partial, "z", scatter_dimension=0, tiled=True)

    unit_terms = [dot(normed2_all, grad_pre, TN).reshape(zs, fc_rows, ff_own)]
    for part in parts:
        unit_terms.append(dot(act_low, grad_all[:, part], TN).reshape(zs, ff_unit, ff_own))
    unit_terms = jnp.concatenate(unit_terms, axis=1).astype(BF16).reshape(-1, ff_own)
    unit_terms, both_all, act_late = together(unit_terms, both_all, act_low)
    normed1_all, attended_all = both_all[:, :width], both_all[:, width:]
    with jax.named_scope("grad_normed2_scatter"):
        grad_normed2, _ = scatter_plane(
            lambda first, count: dot(grad_pre[first : first + count], fc_own, NT),
            rows,
            unit_terms,
        )
    units = over_z(unit_terms)
    dgain2 = jnp.sum(grad_normed2 * unit2, axis=0)
    dshift2 = jnp.sum(grad_normed2, axis=0)
    dproj_bias = jnp.sum(grad_f32, axis=0)
    grad_middle = grad_f32 + norm_back(grad_normed2, unit2, rstd2, gain2)

    grad_branch = grad_middle.astype(BF16)
    dout_bias = jnp.sum(grad_branch.astype(F32), axis=0)
    grad_attended = dot(grad_branch, full_out, NT).astype(BF16)
    dq, dkv_ctx = attention_backward(
        queries, grad_attended, attended, norms, kv_ctx, seg_own, seg_ctx, padding_id
    )
    with jax.named_scope("mlp_out_scatter"):
        mlp_out, _ = scatter_plane(
            lambda first, count: jnp.concatenate(
                [dot(act_late[first : first + count], own, NN) for own in proj_parts], axis=1
            ),
            rows,
            dq,
        )
    dkv = dkv_ctx[halo * rows :]
    for back in range(1, halo + 1):
        pairs = [(i + back, i) for i in range(seqs - back)]
        term = dkv_ctx[(halo - back) * rows : (halo - back + 1) * rows].astype(BF16)
        dkv = dkv + lax.ppermute(term, SEQ, pairs).astype(F32)
    grad_qkv = jnp.concatenate([dq, dkv.astype(BF16)], axis=1)
    grad_normed1 = dot(grad_qkv, full_qkv, NT)
    dgain1 = jnp.sum(grad_normed1 * unit1, axis=0)
    dshift1 = jnp.sum(grad_normed1, axis=0)
    grad_in = grad_middle + norm_back(grad_normed1, unit1, rstd1, gain1)
    with jax.named_scope("input_grad_to_stored"):
        input_grad = to_stored(grad_in.astype(BF16))
    grad_qkv_f32 = grad_qkv.astype(F32)
    dqv_bias = jnp.concatenate(
        [jnp.sum(grad_qkv_f32[:, :width], axis=0), jnp.sum(grad_qkv_f32[:, width + HD :], axis=0)]
    )

    def columns_of_plane(values):
        parts = [values[:, :width].reshape(rows, plane, width // plane)]
        if values.shape[1] > width:
            parts.append(values[:, width:].reshape(rows, plane, -1))
        sent = jnp.concatenate(parts, axis=2).transpose(1, 0, 2)
        cols = sent.shape[2]
        return lax.all_to_all(sent, PLANE, split_axis=0, concat_axis=0, tiled=True).reshape(
            plane * rows, cols
        )

    dout_own = dot(attended_all, columns_of_plane(grad_branch), TN).astype(BF16)
    dqkv_own = dot(normed1_all, columns_of_plane(grad_qkv), TN).astype(BF16)

    first_row_y = y_at * shard
    flipped = (1 - y_at) * shard

    def rows_of_y(partial):
        cols = partial.shape[1]
        if ys == 2:
            kept = lax.dynamic_slice_in_dim(partial, first_row_y, shard, 0)
            return [kept, swap(lax.dynamic_slice_in_dim(partial, flipped, shard, 0), "y")]
        moved = lax.all_to_all(
            partial.reshape(ys, shard, cols), "y", split_axis=0, concat_axis=0, tiled=True
        )
        return [moved[y] for y in range(ys)]

    def near_rep(pieces):
        return pieces + [swap(item, "x") for item in pieces]

    def far_rep(pieces):
        return pieces + [swap(item, "c") for item in pieces]

    def sources(count):
        found = []
        for dc, dx, dy in itertools.product(range(2), range(2), range(count)):
            y = (y_at ^ dy) if ys == 2 else dy
            found.append((y * reps if count > 1 else 0) + (x_at ^ dx) * cs + (c_at ^ dc))
        return jnp.stack(found).astype(jnp.int32)

    proj_near = near_rep([units[fc_rows:]])
    fc_near = near_rep(rows_of_y(units[:fc_rows]))
    result = (middle + mlp_out + proj_shift).astype(BF16)
    result, proj_near, fc_near = together(result, proj_near, fc_near)
    with jax.named_scope("result_to_stored"):
        hidden_out = to_stored(result).astype(BF16)
    head_terms = jnp.concatenate([dqkv_own, dout_own], axis=1)
    heads = over_z(head_terms)
    with jax.named_scope("proj_grad_rows"):
        proj_pieces = far_rep(proj_near)
        dproj_weight = assemble(
            proj_pieces,
            [(p * ff_unit, ff_unit, 0, ff_own, 0, p * ff_own) for p in range(len(parts))],
            [(ff // seqs, width)],
            sources(1) * ff_unit,
        )[0]
    with jax.named_scope("fc_grad_rows"):
        fc_pieces = far_rep(fc_near)
        if small_plane():
            dfc_weight = assemble(
                fc_pieces,
                [(0, shard, z * ff_unit, ff_unit, 0, z * plane * ff_unit) for z in range(zs)],
                [(shard, ff)],
                sources(ys) * ff_unit,
                by_column=True,
            )[0]
        else:
            stacked = jnp.stack(fc_pieces).reshape(plane, shard, zs, ff_unit)
            order = jnp.argsort(sources(ys))
            dfc_weight = (
                stacked[order].transpose(1, 2, 0, 3).reshape(shard, ff).astype(F32)
            )
    dfc_bias = lax.dynamic_update_slice(
        jnp.zeros((zs, ys, reps, ff_unit), F32),
        dfc_bias_own.reshape(zs, 1, 1, ff_unit),
        (0, y_at, q_at, 0),
    ).reshape(ff)
    mids = (dout_bias, dgain2, dshift2, dfc_bias, dproj_bias)
    lasts = (dgain1, dshift1, dqv_bias)

    def reduce_small(items):
        total = jnp.concatenate(items).reshape(-1, HD)
        if small_plane():
            for axis in ("c", "x", "y"):
                total = total + swap(total, axis)
            total = sum([shift(total, "z", away) for away in range(1, zs)], total)
        else:
            total = lax.psum(total, ALL)
        total = total.reshape(-1)
        outs, at = [], 0
        for item in items:
            size = item.shape[0] // seqs
            outs.append(lax.dynamic_slice_in_dim(total, at + seq_at * size, size))
            at += item.shape[0]
        return outs

    mids = reduce_small(mids)
    lasts = reduce_small(lasts)
    heads, dfc_weight, dproj_weight = together(heads, dfc_weight, dproj_weight)
    with jax.named_scope("attention_grad_rows"):
        dout_bias, dgain2, dshift2, dfc_bias, dproj_bias = mids
        dgain1, dshift1, dqv_bias = lasts
        head_pieces = far_rep(near_rep(rows_of_y(heads)))
        q_cols, kv_cols = width // plane, 2 * HD // plane
        if small_plane():
            dqkv_weight, dout_weight = assemble(
                head_pieces,
                [(0, shard, 0, q_cols, 0, 0), (0, shard, q_cols + kv_cols, q_cols, 1, 0)],
                [(shard, qkv_cols), (shard, width)],
                sources(ys) * q_cols,
                by_column=True,
                rolled=(q_cols, kv_cols, 0, width),
            )
        else:
            stacked = jnp.stack(head_pieces)[jnp.argsort(sources(ys))].transpose(1, 0, 2)
            stacked = stacked.astype(F32)
            dq_cols = stacked[:, :, :q_cols].reshape(shard, width)
            dkv_cols = stacked[:, :, q_cols : q_cols + kv_cols].reshape(shard, 2 * HD)
            dqkv_weight = jnp.concatenate([dq_cols, dkv_cols], axis=1)
            dout_weight = stacked[:, :, q_cols + kv_cols :].reshape(shard, width)

    return (
        hidden_out[None],
        input_grad[None],
        dgain1,
        dshift1,
        dqkv_weight,
        dqv_bias,
        dout_weight,
        dout_bias,
        dgain2,
        dshift2,
        dfc_weight,
        dfc_bias,
        dproj_weight,
        dproj_bias,
    )


def solution(mesh):
    seqs, reps = mesh.shape["seq"], mesh.shape["rep"]
    grid = Mesh(mesh.devices.reshape(4, seqs // 4, reps // 2, 2), ALL)
    wide = P(REP, SEQ, None)
    table = P(REP, None)
    vector = P(SEQ)
    matrix = P(SEQ, None)
    return jax.shard_map(
        shards,
        mesh=grid,
        in_specs=(
            wide,
            wide,
            table,
            table,
            vector,
            vector,
            matrix,
            vector,
            matrix,
            vector,
            vector,
            vector,
            matrix,
            vector,
            matrix,
            vector,
        ),
        out_specs=(
            wide,
            wide,
            vector,
            vector,
            matrix,
            vector,
            matrix,
            vector,
            vector,
            vector,
            matrix,
            vector,
            matrix,
            vector,
        ),
        check_vma=False,
    )
```

```python
import functools
import itertools
import math

import jax
import jax.numpy as jnp
from jax import lax
from jax.experimental import pallas as pl
from jax.experimental.pallas import tpu as pltpu
from jax.sharding import Mesh
from jax.sharding import PartitionSpec as P

HD = 128
EPSILON = 1e-05
NEGATIVE = -1e30
SCALE = 1.0 / math.sqrt(HD)
LOG2E = math.log2(math.e)
GELU_C = math.sqrt(2.0 / math.pi)
SEQ = ("z", "y")
REP = ("x", "c")
PLANE = ("y", "x", "c")
ALL = ("z", "y", "x", "c")
BF16 = jnp.bfloat16
F32 = jnp.float32
HEADS_STEP = 4


def dot(left, right, dims):
    return lax.dot_general(left, right, (dims, ((), ())), preferred_element_type=F32)


NN = ((1,), (0,))
NT = ((1,), (1,))
TN = ((0,), (0,))


def attention_bias(seg_own, seg_ctx, padding_id, rows, ctx):
    t = lax.broadcasted_iota(jnp.int32, (rows, ctx), 0)
    u = lax.broadcasted_iota(jnp.int32, (rows, ctx), 1)
    allowed = (seg_own == seg_ctx) & (u <= t + (ctx - rows)) & (seg_own != padding_id)
    return jnp.where(allowed, 0.0, NEGATIVE).astype(F32)


def forward_kernel(padding_id, q_ref, kv_ref, own_ref, ctx_ref, low_ref, att_ref, norm_ref, bias):
    rows, ctx = bias.shape

    @pl.when(pl.program_id(0) == 0)
    def _():
        bias[...] = attention_bias(own_ref[...], ctx_ref[...], padding_id, rows, ctx)

    live = own_ref[...] != padding_id
    keys = kv_ref[:, :HD]
    values = kv_ref[:, HD:]
    for head in range(HEADS_STEP):
        lanes = slice(head * HD, (head + 1) * HD)
        scores = dot(q_ref[:, lanes], keys, NT) * (SCALE * LOG2E) + bias[...]
        top = jnp.max(scores, axis=1, keepdims=True)
        weights = jnp.exp2(scores - top)
        sums = jnp.sum(weights, axis=1, keepdims=True)
        mixed = dot(weights.astype(BF16), values, NN)
        attended = jnp.where(live, mixed / sums, 0.0)
        att_ref[:, lanes] = attended
        low_ref[:, lanes] = attended.astype(BF16)
        norm = jnp.where(live, top + jnp.log2(sums), 0.0)
        norm_ref[:, lanes] = jnp.broadcast_to(norm, (rows, HD))


def attention_forward(queries, kv_ctx, seg_own, seg_ctx, padding_id):
    rows, width = queries.shape
    ctx = kv_ctx.shape[0]
    step = HEADS_STEP * HD
    tile = pl.BlockSpec((rows, step), lambda h: (0, h))
    return pl.pallas_call(
        functools.partial(forward_kernel, padding_id),
        grid=(width // step,),
        in_specs=[
            tile,
            pl.BlockSpec((ctx, 2 * HD), lambda h: (0, 0)),
            pl.BlockSpec((rows, 1), lambda h: (0, 0)),
            pl.BlockSpec((1, ctx), lambda h: (0, 0)),
        ],
        out_specs=[tile, tile, tile],
        out_shape=[
            jax.ShapeDtypeStruct((rows, width), BF16),
            jax.ShapeDtypeStruct((rows, width), F32),
            jax.ShapeDtypeStruct((rows, width), F32),
        ],
        scratch_shapes=[pltpu.VMEM((rows, ctx), F32)],
        compiler_params=pltpu.CompilerParams(vmem_limit_bytes=40 * 1024 * 1024),
        cost_estimate=pl.CostEstimate(
            flops=4 * rows * ctx * width,
            bytes_accessed=12 * rows * width,
            transcendentals=rows * ctx * width // HD,
        ),
        name="attention_forward",
    )(queries, kv_ctx, seg_own, seg_ctx)


def backward_kernel(
    padding_id, q_ref, g_ref, att_ref, norm_ref, kv_ref, own_ref, ctx_ref, dq_ref, dkv_ref, bias
):
    rows, ctx = bias.shape

    @pl.when(pl.program_id(0) == 0)
    def _():
        bias[...] = attention_bias(own_ref[...], ctx_ref[...], padding_id, rows, ctx)
        dkv_ref[...] = jnp.zeros_like(dkv_ref)

    keys = kv_ref[:, :HD]
    values = kv_ref[:, HD:]
    for head in range(HEADS_STEP):
        lanes = slice(head * HD, (head + 1) * HD)
        q = q_ref[:, lanes]
        g = g_ref[:, lanes]
        delta = jnp.sum(g.astype(F32) * att_ref[:, lanes], axis=1, keepdims=True)
        norm = norm_ref[:, head * HD : head * HD + 1]
        scores = dot(q, keys, NT) * (SCALE * LOG2E) + bias[...]
        prob = jnp.exp2(scores - norm)
        grad_prob = dot(g, values, NT)
        grad_scores = (prob * (grad_prob - delta) * SCALE).astype(BF16)
        dq_ref[:, lanes] = dot(grad_scores, keys, NN).astype(BF16)
        dkv_ref[:, :HD] += dot(grad_scores, q, TN)
        dkv_ref[:, HD:] += dot(prob.astype(BF16), g, TN)


def attention_backward(queries, grads, attended, norms, kv_ctx, seg_own, seg_ctx, padding_id):
    rows, width = queries.shape
    ctx = kv_ctx.shape[0]
    step = HEADS_STEP * HD
    tile = pl.BlockSpec((rows, step), lambda h: (0, h))
    whole = pl.BlockSpec((ctx, 2 * HD), lambda h: (0, 0))
    return pl.pallas_call(
        functools.partial(backward_kernel, padding_id),
        grid=(width // step,),
        in_specs=[
            tile,
            tile,
            tile,
            tile,
            whole,
            pl.BlockSpec((rows, 1), lambda h: (0, 0)),
            pl.BlockSpec((1, ctx), lambda h: (0, 0)),
        ],
        out_specs=[tile, whole],
        out_shape=[
            jax.ShapeDtypeStruct((rows, width), BF16),
            jax.ShapeDtypeStruct((ctx, 2 * HD), F32),
        ],
        scratch_shapes=[pltpu.VMEM((rows, ctx), F32)],
        compiler_params=pltpu.CompilerParams(vmem_limit_bytes=48 * 1024 * 1024),
        cost_estimate=pl.CostEstimate(
            flops=10 * rows * ctx * width,
            bytes_accessed=14 * rows * width,
            transcendentals=rows * ctx * width // HD,
        ),
        name="attention_backward",
    )(queries, grads, attended, norms, kv_ctx, seg_own, seg_ctx)


def norm_parts(values):
    center = values - jnp.mean(values, axis=-1, keepdims=True)
    spread = jnp.mean(center * center, axis=-1, keepdims=True)
    rstd = lax.rsqrt(spread + EPSILON)
    return center * rstd, rstd


def norm_back(grad, unit, rstd, gain):
    scaled = grad * gain
    mean_g = jnp.mean(scaled, axis=-1, keepdims=True)
    mean_gu = jnp.mean(scaled * unit, axis=-1, keepdims=True)
    return rstd * (scaled - mean_g - unit * mean_gu)


def gelu_pair(v):
    inner = jnp.tanh(GELU_C * (v + 0.044715 * v * v * v))
    value = 0.5 * v * (1.0 + inner)
    slope = 0.5 * (1.0 + inner) + 0.5 * v * (1.0 - inner * inner) * GELU_C * (
        1.0 + 3.0 * 0.044715 * v * v
    )
    return value, slope


def swap(block, axis):
    return lax.ppermute(block, axis, [(0, 1), (1, 0)])


def pair(block, axis):
    if lax.axis_size(axis) != 2:
        return lax.all_gather(block, axis, axis=0, tiled=False)
    other = swap(block, axis)
    first = lax.axis_index(axis) == 0
    return jnp.stack([jnp.where(first, block, other), jnp.where(first, other, block)])


def small_plane():
    return lax.axis_size("y") == 2


def plane_pieces(block):
    if not small_plane():
        return [lax.all_gather(block, PLANE, axis=0, tiled=True)]
    half = block.shape[0] // 2
    top, low = block[:half], block[half:]
    top_x, low_y = swap(top, "x"), swap(low, "y")
    top_y, low_x = swap(top, "y"), swap(low, "x")
    top_xy, low_yx = swap(top_x, "y"), swap(low_y, "x")
    near = [top, top_y, top_x, top_xy, low, low_x, low_y, low_yx]
    return near + [swap(item, "c") for item in near]


def join_kernel(count, *refs):
    rows = refs[0].shape[0]
    for i in range(count):
        refs[count][i * rows : (i + 1) * rows, :] = refs[i][...]


def join_rows(pieces):
    count = len(pieces)
    if count == 1:
        return pieces[0]
    rows, width = pieces[0].shape
    return pl.pallas_call(
        functools.partial(join_kernel, count),
        grid=(1,),
        in_specs=[pl.BlockSpec((rows, width), lambda i: (0, 0))] * count,
        out_specs=pl.BlockSpec((count * rows, width), lambda i: (0, 0)),
        out_shape=jax.ShapeDtypeStruct((count * rows, width), pieces[0].dtype),
        compiler_params=pltpu.CompilerParams(vmem_limit_bytes=56 * 1024 * 1024),
        cost_estimate=pl.CostEstimate(
            flops=0, bytes_accessed=4 * count * rows * width, transcendentals=0
        ),
        name="join_rows",
    )(*pieces)


def gather_plane(block):
    return join_rows(plane_pieces(block))


def scatter_plane(partial, rows, hold=None):
    total = rows * lax.axis_size("y") * lax.axis_size("x") * lax.axis_size("c")
    if not small_plane():
        return lax.psum_scatter(
            partial(0, total).astype(BF16), PLANE, scatter_dimension=0, tiled=True
        ).astype(F32), hold
    side = total // 2
    got = swap(partial(side, side).astype(BF16), "c")
    both = (partial(0, side) + got.astype(F32)).astype(BF16)
    if hold is not None:
        both, _ = together(both, hold)
    top, low = both[: side // 2], both[side // 2 :]
    got_top, got_low = swap(top[rows:], "x"), swap(low[rows:], "y")
    top = (top[:rows].astype(F32) + got_top.astype(F32)).astype(BF16)
    low = (low[:rows].astype(F32) + got_low.astype(F32)).astype(BF16)
    half = rows // 2
    got_top, got_low = swap(top[half:], "y"), swap(low[half:], "x")
    sums = jnp.concatenate(
        [
            top[:half].astype(F32) + got_top.astype(F32),
            low[:half].astype(F32) + got_low.astype(F32),
        ],
        axis=0,
    )
    return sums, got_low


def shift(block, axis, by):
    count = math.prod(lax.axis_size(a) for a in ([axis] if isinstance(axis, str) else axis))
    return lax.ppermute(block, axis, [(i, (i + by) % count) for i in range(count)])


def place_kernel(count, parts, offsets, *refs):
    out = refs[count]
    for i in range(count):
        rows = refs[i].shape[0] // parts
        for j in range(parts):
            start = pl.multiple_of(offsets[i * parts + j], rows)
            out[pl.ds(start, rows), :] = refs[i][j * rows : (j + 1) * rows, :]


def place_rows(pieces, parts, offsets):
    count = len(pieces)
    rows, width = pieces[0].shape
    return pl.pallas_call(
        functools.partial(place_kernel, count, parts),
        grid_spec=pltpu.PrefetchScalarGridSpec(
            num_scalar_prefetch=1,
            grid=(1,),
            in_specs=[pl.BlockSpec((rows, width), lambda i, at: (0, 0))] * count,
            out_specs=pl.BlockSpec((count * rows, width), lambda i, at: (0, 0)),
        ),
        out_shape=jax.ShapeDtypeStruct((count * rows, width), pieces[0].dtype),
        compiler_params=pltpu.CompilerParams(vmem_limit_bytes=56 * 1024 * 1024),
        cost_estimate=pl.CostEstimate(
            flops=0, bytes_accessed=4 * count * rows * width, transcendentals=0
        ),
        name="place_rows",
    )(offsets, *pieces)


def assemble_kernel(count, slices, by_column, rolled, offsets, *refs):
    outs = refs[count:]
    if rolled is not None:
        total = jnp.zeros((refs[0].shape[0], 2 * HD), F32)
    for i in range(count):
        for row, rows, first, cols, target, base in slices:
            values = refs[i][row : row + rows, first : first + cols].astype(F32)
            if by_column:
                start = pl.multiple_of(offsets[i] + base, HD)
                outs[target][:, pl.ds(start, cols)] = values
            else:
                start = pl.multiple_of(offsets[i], rows)
                outs[target][pl.ds(start, rows), base : base + cols] = values
        if rolled is not None:
            first, wide, target, at = rolled
            narrow = refs[i][:, first : first + wide].astype(F32)
            padded = jnp.concatenate(
                [narrow, jnp.zeros((narrow.shape[0], 2 * HD - wide), F32)], axis=1
            )
            total = total + pltpu.roll(padded, offsets[i] * wide // slices[0][3], 1)
    if rolled is not None:
        outs[target][:, at : at + 2 * HD] = total


def assemble(pieces, slices, shapes, offsets, by_column=False, rolled=None):
    count = len(pieces)
    rows, width = pieces[0].shape
    return pl.pallas_call(
        functools.partial(assemble_kernel, count, slices, by_column, rolled),
        grid_spec=pltpu.PrefetchScalarGridSpec(
            num_scalar_prefetch=1,
            grid=(1,),
            in_specs=[pl.BlockSpec((rows, width), lambda i, at: (0, 0))] * count,
            out_specs=[pl.BlockSpec(shape, lambda i, at: (0, 0)) for shape in shapes],
        ),
        out_shape=[jax.ShapeDtypeStruct(shape, F32) for shape in shapes],
        compiler_params=pltpu.CompilerParams(vmem_limit_bytes=56 * 1024 * 1024),
        cost_estimate=pl.CostEstimate(
            flops=0, bytes_accessed=6 * count * rows * width, transcendentals=0
        ),
        name="assemble_rows",
    )(offsets, *pieces)


def together(*values):
    return lax.optimization_barrier(values)


def spread_near(column):
    side = column.shape[0] // 2
    near = []
    for part in range(2):
        own = column[part * side : (part + 1) * side]
        one, two = ("x", "y") if part == 0 else ("y", "x")
        near += [own, swap(own, one), swap(own, two)]
    return near


def spread_far(near):
    zs = lax.axis_size("z")
    y, x, c = (lax.axis_index(a) for a in PLANE)
    rows = near[0].shape[0] // (zs // 2)
    pieces, offsets = [], []
    for part in range(2):
        one, two = ("x", "y") if part == 0 else ("y", "x")
        own, by_one, by_two = near[3 * part : 3 * part + 3]
        for item, at_one, at_two in (
            (own, 0, 0),
            (by_one, 1, 0),
            (by_two, 0, 1),
            (swap(by_one, two), 1, 1),
        ):
            dx, dy = (at_one, at_two) if one == "x" else (at_two, at_one)
            for dc in range(2):
                pieces.append(swap(item, "c") if dc else item)
                source = ((y ^ dy) * 2 + (x ^ dx)) * 2 + (c ^ dc)
                for z in range(zs // 2):
                    offsets.append(((part * (zs // 2) + z) * 8 + source) * rows)
    return place_rows(pieces, zs // 2, jnp.stack(offsets).astype(jnp.int32))


def shards(
    hidden_in,
    out_grad,
    segment_ids,
    row_position,
    gain_first,
    shift_first,
    qkv_weight,
    qv_bias,
    out_weight,
    out_bias,
    gain_second,
    shift_second,
    fc_weight,
    fc_bias,
    proj_weight,
    proj_bias,
):
    zs, ys, xs, cs = (lax.axis_size(a) for a in ALL)
    reps = xs * cs
    plane = ys * reps
    seqs = zs * ys
    z_at, y_at, x_at, c_at = (lax.axis_index(a) for a in ALL)
    q_at = x_at * cs + c_at
    f_at = y_at * reps + q_at
    seq_at = z_at * ys + y_at
    rows = hidden_in.shape[1]
    width = hidden_in.shape[2]
    window = rows * seqs
    capacity = 2 * rows // seqs
    halo = max(1, seqs // 4)
    ctx = (halo + 1) * rows
    padding_id = max(8, window // 256) - 1
    qkv_cols = qkv_weight.shape[1]
    ff = fc_weight.shape[1]
    ff_unit = ff // seqs // reps
    ff_own = zs * ff_unit
    shard = width // seqs

    def fc_columns(y):
        picked = []
        for z in range(zs):
            start = ((z * ys + y) * reps + q_at) * ff_unit
            picked.append(lax.dynamic_slice_in_dim(fc_weight, start, ff_unit, 1))
        return jnp.concatenate(picked, axis=1)

    if ys == 2:
        fc_mine, fc_other = fc_columns(y_at), swap(fc_columns(1 - y_at), "y")
        fc_pair = jnp.concatenate(
            [jnp.where(y_at == 0, fc_mine, fc_other), jnp.where(y_at == 0, fc_other, fc_mine)]
        )
    else:
        fc_pair = lax.all_to_all(
            jnp.stack([fc_columns(y) for y in range(ys)]), "y", 0, 0, tiled=True
        ).reshape(ys * shard, ff_own)

    places = row_position[0]
    segments = segment_ids[0]
    targets = (places // rows).reshape(seqs, rows)
    earlier = (
        lax.broadcasted_iota(jnp.int32, (rows, rows), 1)
        < lax.broadcasted_iota(jnp.int32, (rows, rows), 0)
    )
    same = (targets[:, :, None] == targets[:, None, :]) & earlier[None]
    ranks = jnp.sum(same.astype(jnp.int32), axis=2).reshape(window)
    first_row = seq_at * rows
    slots = seqs * capacity
    send_slots = lax.dynamic_slice_in_dim(places // rows * capacity + ranks, first_row, rows)
    arrive_slots = jnp.arange(window, dtype=jnp.int32) // rows * capacity + ranks
    own_places = first_row + jnp.arange(rows, dtype=jnp.int32)
    recv_slots = jnp.sum(
        jnp.where(places[None, :] == own_places[:, None], arrive_slots[None, :], 0), axis=1
    )
    slot_ids = jnp.arange(slots, dtype=jnp.int32)
    pick_send = (send_slots[:, None] == slot_ids[None, :]).astype(BF16)
    pick_recv = (recv_slots[:, None] == slot_ids[None, :]).astype(BF16)

    def exchange_first(values):
        wide = capacity + extra
        wide_ids = jnp.arange(seqs * wide, dtype=jnp.int32)
        send_wide = send_slots // capacity * wide + send_slots % capacity
        recv_wide = recv_slots // capacity * wide + recv_slots % capacity
        pick_rows = (send_wide[:, None] == wide_ids[None, :]).astype(BF16)
        pick_small = (wide_ids % wide - capacity)[None, :] == jnp.arange(extra)[:, None]
        packed = dot(
            jnp.concatenate([pick_rows, pick_small.astype(BF16)], axis=0),
            jnp.concatenate([values, small_rows], axis=0),
            TN,
        )
        packed = packed.astype(BF16).reshape(seqs, wide, width)
        moved = lax.all_to_all(packed, SEQ, split_axis=0, concat_axis=0, tiled=True)
        return moved, recv_wide, wide_ids

    def arrive_first(moved, recv_wide, wide_ids):
        pick_wide = (recv_wide[:, None] == wide_ids[None, :]).astype(BF16)
        every = moved[:, capacity:].reshape(seqs, extra * width)[:, : small.shape[0]]
        return dot(pick_wide, moved.reshape(wide_ids.shape[0], width), NN), every.astype(F32)

    def exchange(values, pick_out, pick_in):
        packed = dot(pick_out, values, TN).astype(BF16).reshape(seqs, capacity, values.shape[1])
        moved = lax.all_to_all(packed, SEQ, split_axis=0, concat_axis=0, tiled=True)
        return dot(pick_in, moved.reshape(slots, values.shape[1]), NN)

    def to_places(values):
        return exchange(values, pick_send, pick_recv)

    def to_stored(values):
        return exchange(values, pick_recv, pick_send)

    vectors = (
        gain_first,
        shift_first,
        qv_bias,
        out_bias,
        gain_second,
        shift_second,
        fc_bias,
        proj_bias,
    )
    small = jnp.concatenate(vectors)
    extra = -(-small.shape[0] // (8 * width)) * 8
    small_rows = jnp.pad(small, (0, extra * width - small.shape[0])).reshape(extra, width)

    def quarter(weight):
        size = weight.shape[0] // reps
        return lax.dynamic_slice_in_dim(weight, q_at * size, size, 0)

    proj_rows = quarter(proj_weight)
    parts = [slice(p * ff_own, (p + 1) * ff_own) for p in range(width // ff_own)]
    fc_rows = ys * shard
    units_part = jnp.concatenate([fc_pair] + [proj_rows[:, part] for part in parts], axis=0)
    with jax.named_scope("attention_weights"):
        if small_plane():
            stored, quarters = together(
                hidden_in[0],
                jnp.concatenate([quarter(qkv_weight), quarter(out_weight)], axis=1),
            )
            columns = lax.all_gather(quarters, "z", axis=0, tiled=True)
        else:
            stored = hidden_in[0]
            columns = lax.all_gather(quarter(qkv_weight), ALL, axis=0, tiled=True)
    with jax.named_scope("hidden_to_places"):
        moved, *picks = exchange_first(stored)
    units_part, grad_stored, columns, moved = together(
        units_part, out_grad[0], columns, moved
    )
    with jax.named_scope("units_gather"):
        hidden_units = lax.all_gather(units_part, "z", axis=0, tiled=False)

    with jax.named_scope("hidden_to_places"):
        inputs, small_all = arrive_first(moved, *picks)
    if small_plane():
        qkv_near = spread_near(columns[:, :qkv_cols])
        out_column, *qkv_near = together(columns[:, qkv_cols:], *qkv_near)
        with jax.named_scope("qkv_gather"):
            full_qkv = spread_far(qkv_near)
        with jax.named_scope("out_gather"):
            full_out = spread_far(spread_near(out_column))
    else:
        full_qkv = columns
        full_out = lax.all_gather(quarter(out_weight), ALL, axis=0, tiled=True)
    wholes = []
    at = 0
    for item in vectors:
        wholes.append(small_all[:, at : at + item.shape[0]].reshape(-1))
        at += item.shape[0]
    gain1, shift1, qv_full, out_shift, gain2, shift2, fc_shift, proj_shift = wholes
    fc_shift_own = lax.dynamic_slice(
        fc_shift.reshape(zs, ys, reps, ff_unit), (0, y_at, q_at, 0), (zs, 1, 1, ff_unit)
    ).reshape(ff_own)

    unit1, rstd1 = norm_parts(inputs)
    normed1 = (unit1 * gain1 + shift1).astype(BF16)
    projected = dot(normed1, full_qkv, NN)
    queries = (projected[:, :width] + qv_full[:width]).astype(BF16)
    kv_shift = jnp.concatenate([jnp.zeros((HD,), F32), qv_full[width:]])
    kv_own = (projected[:, width:] + kv_shift).astype(BF16)
    blocks = []
    for back in range(halo, 0, -1):
        pairs = [(i, i + back) for i in range(seqs - back)]
        blocks.append(lax.ppermute(kv_own, SEQ, pairs))
    kv_ctx = jnp.concatenate(blocks + [kv_own], axis=0)
    with jax.named_scope("grad_to_places"):
        grad_f32 = to_places(grad_stored)
    queries, grad_f32 = together(queries, grad_f32)
    seg_own = lax.dynamic_slice_in_dim(segments, first_row, rows)[:, None]
    seg_padded = jnp.concatenate([jnp.full((halo * rows,), -1, jnp.int32), segments])
    seg_ctx = lax.dynamic_slice_in_dim(seg_padded, first_row, ctx)[None, :]
    attended_low, attended, norms = attention_forward(
        queries, kv_ctx, seg_own, seg_ctx, padding_id
    )
    grad_low = grad_f32.astype(BF16)
    with jax.named_scope("grad_gather"):
        grad_all = gather_plane(grad_low)
    attended_low, grad_all = together(attended_low, grad_all)
    middle = inputs + (dot(attended_low, full_out, NN) + out_shift)

    unit2, rstd2 = norm_parts(middle)
    normed2 = (unit2 * gain2 + shift2).astype(BF16)
    with jax.named_scope("normed2_gather"):
        normed2_all = gather_plane(normed2)
    with jax.named_scope("both_gather"):
        both_low, normed2_all = together(
            jnp.concatenate([normed1, attended_low], axis=1), normed2_all
        )
        both_all = lax.all_gather(both_low, PLANE, axis=0, tiled=True)
    fc_own = hidden_units[:, :fc_rows].reshape(width, ff_own)
    proj_parts = [
        hidden_units[:, fc_rows + p * ff_unit : fc_rows + (p + 1) * ff_unit].reshape(ff_own, ff_own)
        for p in range(len(parts))
    ]

    pre_act = dot(normed2_all, fc_own, NN) + fc_shift_own
    act, slope = gelu_pair(pre_act)
    act_low = act.astype(BF16)
    grad_act = sum(dot(grad_all[:, part], own, NT) for part, own in zip(parts, proj_parts))
    grad_pre = (grad_act * slope).astype(BF16)
    dfc_bias_own = jnp.sum(grad_pre.astype(F32), axis=0)

    def over_z(partial):
        return lax.psum_scatter(partial, "z", scatter_dimension=0, tiled=True)

    unit_terms = [dot(normed2_all, grad_pre, TN).reshape(zs, fc_rows, ff_own)]
    for part in parts:
        unit_terms.append(dot(act_low, grad_all[:, part], TN).reshape(zs, ff_unit, ff_own))
    unit_terms = jnp.concatenate(unit_terms, axis=1).astype(BF16).reshape(-1, ff_own)
    unit_terms, both_all, act_late = together(unit_terms, both_all, act_low)
    normed1_all, attended_all = both_all[:, :width], both_all[:, width:]
    with jax.named_scope("grad_normed2_scatter"):
        grad_normed2, _ = scatter_plane(
            lambda first, count: dot(grad_pre[first : first + count], fc_own, NT),
            rows,
            unit_terms,
        )
    units = over_z(unit_terms)
    dgain2 = jnp.sum(grad_normed2 * unit2, axis=0)
    dshift2 = jnp.sum(grad_normed2, axis=0)
    dproj_bias = jnp.sum(grad_f32, axis=0)
    grad_middle = grad_f32 + norm_back(grad_normed2, unit2, rstd2, gain2)

    grad_branch = grad_middle.astype(BF16)
    dout_bias = jnp.sum(grad_branch.astype(F32), axis=0)
    grad_attended = dot(grad_branch, full_out, NT).astype(BF16)
    dq, dkv_ctx = attention_backward(
        queries, grad_attended, attended, norms, kv_ctx, seg_own, seg_ctx, padding_id
    )
    with jax.named_scope("mlp_out_scatter"):
        mlp_out, _ = scatter_plane(
            lambda first, count: jnp.concatenate(
                [dot(act_late[first : first + count], own, NN) for own in proj_parts], axis=1
            ),
            rows,
            dq,
        )
    dkv = dkv_ctx[halo * rows :]
    for back in range(1, halo + 1):
        pairs = [(i + back, i) for i in range(seqs - back)]
        term = dkv_ctx[(halo - back) * rows : (halo - back + 1) * rows].astype(BF16)
        dkv = dkv + lax.ppermute(term, SEQ, pairs).astype(F32)
    grad_qkv = jnp.concatenate([dq, dkv.astype(BF16)], axis=1)
    grad_normed1 = dot(grad_qkv, full_qkv, NT)
    dgain1 = jnp.sum(grad_normed1 * unit1, axis=0)
    dshift1 = jnp.sum(grad_normed1, axis=0)
    grad_in = grad_middle + norm_back(grad_normed1, unit1, rstd1, gain1)
    with jax.named_scope("input_grad_to_stored"):
        input_grad = to_stored(grad_in.astype(BF16))
    grad_qkv_f32 = grad_qkv.astype(F32)
    dqv_bias = jnp.concatenate(
        [jnp.sum(grad_qkv_f32[:, :width], axis=0), jnp.sum(grad_qkv_f32[:, width + HD :], axis=0)]
    )

    def columns_of_plane(values):
        parts = [values[:, :width].reshape(rows, plane, width // plane)]
        if values.shape[1] > width:
            parts.append(values[:, width:].reshape(rows, plane, -1))
        sent = jnp.concatenate(parts, axis=2).transpose(1, 0, 2)
        cols = sent.shape[2]
        return lax.all_to_all(sent, PLANE, split_axis=0, concat_axis=0, tiled=True).reshape(
            plane * rows, cols
        )

    dout_own = dot(attended_all, columns_of_plane(grad_branch), TN).astype(BF16)
    dqkv_own = dot(normed1_all, columns_of_plane(grad_qkv), TN).astype(BF16)

    first_row_y = y_at * shard
    flipped = (1 - y_at) * shard

    def rows_of_y(partial):
        cols = partial.shape[1]
        if ys == 2:
            kept = lax.dynamic_slice_in_dim(partial, first_row_y, shard, 0)
            return [kept, swap(lax.dynamic_slice_in_dim(partial, flipped, shard, 0), "y")]
        moved = lax.all_to_all(
            partial.reshape(ys, shard, cols), "y", split_axis=0, concat_axis=0, tiled=True
        )
        return [moved[y] for y in range(ys)]

    def near_rep(pieces):
        return pieces + [swap(item, "x") for item in pieces]

    def far_rep(pieces):
        return pieces + [swap(item, "c") for item in pieces]

    def sources(count):
        found = []
        for dc, dx, dy in itertools.product(range(2), range(2), range(count)):
            y = (y_at ^ dy) if ys == 2 else dy
            found.append((y * reps if count > 1 else 0) + (x_at ^ dx) * cs + (c_at ^ dc))
        return jnp.stack(found).astype(jnp.int32)

    proj_near = near_rep([units[fc_rows:]])
    fc_near = near_rep(rows_of_y(units[:fc_rows]))
    result = (middle + mlp_out + proj_shift).astype(BF16)
    result, proj_near, fc_near = together(result, proj_near, fc_near)
    with jax.named_scope("result_to_stored"):
        hidden_out = to_stored(result).astype(BF16)
    head_terms = jnp.concatenate([dqkv_own, dout_own], axis=1)
    heads = over_z(head_terms)
    with jax.named_scope("proj_grad_rows"):
        proj_pieces = far_rep(proj_near)
        dproj_weight = assemble(
            proj_pieces,
            [(p * ff_unit, ff_unit, 0, ff_own, 0, p * ff_own) for p in range(len(parts))],
            [(ff // seqs, width)],
            sources(1) * ff_unit,
        )[0]
    with jax.named_scope("fc_grad_rows"):
        fc_pieces = far_rep(fc_near)
        if small_plane():
            dfc_weight = assemble(
                fc_pieces,
                [(0, shard, z * ff_unit, ff_unit, 0, z * plane * ff_unit) for z in range(zs)],
                [(shard, ff)],
                sources(ys) * ff_unit,
                by_column=True,
            )[0]
        else:
            stacked = jnp.stack(fc_pieces).reshape(plane, shard, zs, ff_unit)
            order = jnp.argsort(sources(ys))
            dfc_weight = (
                stacked[order].transpose(1, 2, 0, 3).reshape(shard, ff).astype(F32)
            )
    dfc_bias = lax.dynamic_update_slice(
        jnp.zeros((zs, ys, reps, ff_unit), F32),
        dfc_bias_own.reshape(zs, 1, 1, ff_unit),
        (0, y_at, q_at, 0),
    ).reshape(ff)
    mids = (dout_bias, dgain2, dshift2, dfc_bias, dproj_bias)
    lasts = (dgain1, dshift1, dqv_bias)

    def reduce_small(items):
        total = jnp.concatenate(items).reshape(-1, HD)
        if small_plane():
            for axis in ("c", "x", "y"):
                total = total + swap(total, axis)
            total = sum([shift(total, "z", away) for away in range(1, zs)], total)
        else:
            total = lax.psum(total, ALL)
        total = total.reshape(-1)
        outs, at = [], 0
        for item in items:
            size = item.shape[0] // seqs
            outs.append(lax.dynamic_slice_in_dim(total, at + seq_at * size, size))
            at += item.shape[0]
        return outs

    mids = reduce_small(mids)
    lasts = reduce_small(lasts)
    heads, dfc_weight, dproj_weight = together(heads, dfc_weight, dproj_weight)
    with jax.named_scope("attention_grad_rows"):
        dout_bias, dgain2, dshift2, dfc_bias, dproj_bias = mids
        dgain1, dshift1, dqv_bias = lasts
        head_pieces = far_rep(near_rep(rows_of_y(heads)))
        q_cols, kv_cols = width // plane, 2 * HD // plane
        if small_plane():
            dqkv_weight, dout_weight = assemble(
                head_pieces,
                [(0, shard, 0, q_cols, 0, 0), (0, shard, q_cols + kv_cols, q_cols, 1, 0)],
                [(shard, qkv_cols), (shard, width)],
                sources(ys) * q_cols,
                by_column=True,
                rolled=(q_cols, kv_cols, 0, width),
            )
        else:
            stacked = jnp.stack(head_pieces)[jnp.argsort(sources(ys))].transpose(1, 0, 2)
            stacked = stacked.astype(F32)
            dq_cols = stacked[:, :, :q_cols].reshape(shard, width)
            dkv_cols = stacked[:, :, q_cols : q_cols + kv_cols].reshape(shard, 2 * HD)
            dqkv_weight = jnp.concatenate([dq_cols, dkv_cols], axis=1)
            dout_weight = stacked[:, :, q_cols + kv_cols :].reshape(shard, width)

    return (
        hidden_out[None],
        input_grad[None],
        dgain1,
        dshift1,
        dqkv_weight,
        dqv_bias,
        dout_weight,
        dout_bias,
        dgain2,
        dshift2,
        dfc_weight,
        dfc_bias,
        dproj_weight,
        dproj_bias,
    )


def solution(mesh):
    seqs, reps = mesh.shape["seq"], mesh.shape["rep"]
    grid = Mesh(mesh.devices.reshape(4, seqs // 4, reps // 2, 2), ALL)
    wide = P(REP, SEQ, None)
    table = P(REP, None)
    vector = P(SEQ)
    matrix = P(SEQ, None)
    return jax.shard_map(
        shards,
        mesh=grid,
        in_specs=(
            wide,
            wide,
            table,
            table,
            vector,
            vector,
            matrix,
            vector,
            matrix,
            vector,
            vector,
            vector,
            matrix,
            vector,
            matrix,
            vector,
        ),
        out_specs=(
            wide,
            wide,
            vector,
            vector,
            matrix,
            vector,
            matrix,
            vector,
            vector,
            vector,
            matrix,
            vector,
            matrix,
            vector,
        ),
        check_vma=False,
    )
```
